256 devices in a mesh: band: 4 (over z_lo), rail: 64 (over x, z_hi, y, core).
Axes of the slice: x: 4, y: 4, z: 8 (z_hi: 2, z_lo: 4; z = z_hi * 4 + z_lo), core: 2. Of those that a mesh axis runs over, the one named last changes fastest.
Arguments:
- features: bfloat16 [64, 64, 96, 256], P('rail', 'band'), may hold values from -6 to 6
- first_kernel: bfloat16 [3, 3, 256, 256], replicated, may hold values from -0.125 to 0.125
- second_kernel: bfloat16 [3, 3, 256, 256], replicated, may hold values from -0.125 to 0.125
- classifier: bfloat16 [256, 3], replicated, may hold values from -0.011962891 to 0.011962891
- class_bias: float32 [3], replicated, may hold values from -0.04 to 0.04
- labels: int32 [64, 64, 96], P('rail', 'band'), may hold values from 0 to 2
Outputs:
- grad_features: bfloat16 [64, 64, 96, 256], P('rail', 'band')
- grad_first: float32 [3, 3, 256, 256], replicated
- grad_second: float32 [3, 3, 256, 256], replicated
- grad_classifier: float32 [256, 3], replicated
- grad_bias: float32 [3], replicated
The draws below stay inside these ranges and needn't reach their ends.
All inputs are finite; a program needn't handle non-finite values.
Results may differ from the reference program's by a relative error of at most 0.013.
Values may be sent and summed in bfloat16 or wider, within the bound.
No kernel may reach another device: no remote copies, remote signals or barrier semaphores. Data moves between devices by JAX's collectives and lax.ppermute only.
A program may use at most 64 MiB of HBM per device.

```python
import jax
import jax.numpy as jnp
from jax import lax

C = 256
CLASSES = 3
COLS = 96
ROWS = 64
IMAGES = 64
PIXELS = 393216


def with_ends(entries, rng, least, high):
    longest = entries.shape.index(max(entries.shape))
    spots = []
    for shift in (0, 1):
        where = [jax.random.randint(jax.random.fold_in(rng, axis), (), 0, length) for axis, length in enumerate(entries.shape)]
        where[longest] = (where[longest] + shift) % entries.shape[longest]
        spots.append(tuple(where))
    return entries.at[spots[0]].set(least).at[spots[1]].set(high)


def shard_levels(key, shape, pieces, low, high):
    def one(dim, blocks):
        heights = jax.random.uniform(jax.random.fold_in(jax.random.fold_in(key, 6), dim), (blocks,), jnp.float32, low / len(pieces), high / len(pieces))
        return jnp.repeat(jnp.exp(heights), shape[dim] // blocks).reshape((-1,) + (1,) * (len(shape) - dim - 1))

    loudness = one(*pieces[0])
    for cut in pieces[1:]:
        loudness = loudness * one(*cut)
    return loudness


def centred(rng, extent, scale, limit, pieces=(), held_as=jnp.bfloat16):
    array = scale * jax.random.normal(rng, extent, jnp.float32)
    if pieces:
        array = array * shard_levels(rng, extent, pieces, -0.22, 0.18)
    return jnp.clip(array, -limit, limit).astype(held_as)


def setup_inputs(seed: int = 0) -> dict:
    key_of = jax.random.split(jax.random.key(seed), 7)
    return {
        "features": centred(key_of[0], (IMAGES, ROWS, COLS, C), 1.0, 6.0, ((0, 64), (1, 4))),
        "first_kernel": centred(key_of[1], (3, 3, C, C), (9 * C) ** -0.5, 0.125),
        "second_kernel": centred(key_of[2], (3, 3, C, C), (9 * C) ** -0.5, 0.125),
        "classifier": centred(key_of[3], (C, CLASSES), 0.002, 0.011962891),
        "class_bias": centred(key_of[4], (CLASSES,), 0.01, 0.04, (), jnp.float32),
        "labels": with_ends(jax.random.randint(key_of[5], (IMAGES, ROWS, COLS), 0, 3), jax.random.fold_in(key_of[5], 1), 0, 2).astype(jnp.int32),
    }


def convolve(field, kernel):
    return lax.conv_general_dilated(field.astype(jnp.float32), kernel.astype(jnp.float32), (1, 1), 'SAME', dimension_numbers=('NHWC', 'HWIO', 'NHWC'), precision=lax.Precision.HIGHEST)

def flipped(kernel):
    return jnp.transpose(kernel[::-1, ::-1], (0, 1, 3, 2))

def silu_slope(value):
    sig = jax.nn.sigmoid(value)
    return sig * (1.0 + value * (1.0 - sig))

def kernel_grad(source, grad):
    padded = jnp.pad(source.astype(jnp.float32), ((0, 0), (1, 1), (1, 1), (0, 0)))
    gradf = grad.astype(jnp.float32)
    taps = []
    for row_tap in range(3):
        line = []
        for col_tap in range(3):
            window = padded[:, row_tap:row_tap + ROWS, col_tap:col_tap + COLS, :]
            line.append(jnp.einsum('nhwc,nhwd->cd', window, gradf, precision=lax.Precision.HIGHEST))
        taps.append(jnp.stack(line))
    return jnp.stack(taps)

def reference(features, first_kernel, second_kernel, classifier, class_bias, labels):
    first_pre = convolve(features, first_kernel)
    first_act = jax.nn.silu(first_pre).astype(jnp.bfloat16)
    second_pre = convolve(first_act, second_kernel)
    second_act = jax.nn.silu(second_pre).astype(jnp.bfloat16)
    flat_act = second_act.reshape(-1, C)
    logits = jnp.dot(flat_act, classifier, preferred_element_type=jnp.float32) + class_bias
    onehot = (labels.reshape(-1)[:, None] == jnp.arange(CLASSES, dtype=jnp.int32)[None, :]).astype(jnp.float32)
    dlogits = (jax.nn.softmax(logits, axis=-1) - onehot) * float(PIXELS) ** (-0.5)
    grad_bias = lax.optimization_barrier(jnp.sum(dlogits, axis=0))
    grad_classifier = jnp.dot(flat_act.astype(jnp.float32).T, dlogits, precision=lax.Precision.HIGHEST)
    back = jnp.dot(dlogits, classifier.astype(jnp.float32).T, precision=lax.Precision.HIGHEST).reshape(second_pre.shape)
    second_grad = (back * silu_slope(second_pre)).astype(jnp.bfloat16)
    grad_second = kernel_grad(first_act, second_grad)
    first_grad = (convolve(second_grad, flipped(second_kernel)) * silu_slope(first_pre)).astype(jnp.bfloat16)
    grad_first = kernel_grad(features, first_grad)
    grad_features = convolve(first_grad, flipped(first_kernel)).astype(jnp.bfloat16)
    return (grad_features, grad_first, grad_second, grad_classifier, grad_bias)
```

```python
import jax
import jax.numpy as jnp
from jax import lax
from jax.experimental import pallas as pl
from jax.experimental.pallas import tpu as pltpu
from jax.sharding import Mesh, PartitionSpec as P

ROWS = 16
COLS = 96
CH = 256
F32 = jnp.float32
BF16 = jnp.bfloat16
PAR = (((0,), (0,)), ((), ()))


def conv_rows(wide, start, count, kernel):
    patch = jnp.concatenate(
        [wide[pl.ds(pl.multiple_of(start + a * COLS, COLS), count * COLS), :] for a in range(3)],
        axis=1,
    )
    out = jnp.dot(patch, kernel[...], preferred_element_type=F32)
    return out.reshape(count, COLS, CH)


def store_wide(wide, start, rows):
    count = rows.shape[0]
    col = lax.broadcasted_iota(jnp.int32, rows.shape, 1)
    left = jnp.where(col == 0, 0.0, pltpu.roll(rows, 1, 1))
    right = jnp.where(col == COLS - 1, 0.0, pltpu.roll(rows, COLS - 1, 1))
    at = pl.ds(pl.multiple_of(start, COLS), count * COLS)
    wide[at, 0:CH] = left.astype(BF16).reshape(count * COLS, CH)
    wide[at, CH:2 * CH] = rows.astype(BF16).reshape(count * COLS, CH)
    wide[at, 2 * CH:3 * CH] = right.astype(BF16).reshape(count * COLS, CH)


def sigmoid(value):
    return 0.5 * jnp.tanh(0.5 * value) + 0.5


def keep_rows(rows, first, height):
    parts = []
    for r in range(rows.shape[0]):
        inside = jnp.logical_and(first + r >= 0, first + r < height)
        parts.append(rows[r] * jnp.where(inside, 1.0, 0.0))
    return jnp.stack(parts)


def make_main(height, scale, r1=2, r2=4, rt=2):
    def main(band_ref, f_ref, k1, k2, k2t, cls, bias, lab, own, g1, g2, small, fg,
             fw, aw, sw, gt, slope):
        base = band_ref[0] * ROWS
        n1, n2, nt = 22 // r1, 20 // r2, 18 // rt

        def widen(t, c):
            at = t * (2 * COLS)
            rows = f_ref[pl.ds(pl.multiple_of(at, COLS), 2 * COLS), :].astype(F32)
            store_wide(fw, at, rows.reshape(2, COLS, CH))
            return c

        lax.fori_loop(0, 12, widen, 0)

        def first(t, c):
            at = t * (r1 * COLS)
            v = conv_rows(fw, at, r1, k1)
            s = sigmoid(v)
            slope[pl.ds(pl.multiple_of(at, COLS), r1 * COLS), :] = (
                s * (1.0 + v * (1.0 - s))
            ).reshape(r1 * COLS, CH)
            store_wide(aw, at, keep_rows(v * s, base - 3 + t * r1, height))
            return c

        lax.fori_loop(0, n1, first, 0)

        small[...] = jnp.zeros_like(small)
        lane = lax.broadcasted_iota(jnp.int32, (8, CH), 1)

        def second(t, c):
            at = t * (r2 * COLS)
            v = conv_rows(aw, at, r2, k2)
            s = sigmoid(v)
            act = (v * s).astype(BF16).reshape(r2 * COLS, CH)
            logit = lax.dot_general(
                cls[...], act, (((1,), (1,)), ((), ())), preferred_element_type=F32
            )
            rows = [logit[k:k + 1, :] + bias[k:k + 1, 0:1] for k in range(3)]
            top = jnp.maximum(jnp.maximum(rows[0], rows[1]), rows[2])
            ex = [jnp.exp(row - top) for row in rows]
            den = ex[0] + ex[1] + ex[2]
            label = lab[t]
            mine = own[t]
            dl = [(ex[k] / den - jnp.where(label == k, 1.0, 0.0)) * scale for k in range(3)]
            hi = [d.astype(BF16).astype(F32) for d in dl]
            lo = [d - h for d, h in zip(dl, hi)]
            zero = jnp.zeros((10, r2 * COLS), F32)
            pack = jnp.concatenate(hi + lo + [zero], axis=0)
            back = lax.dot_general(pack.astype(BF16), cls[...], PAR, preferred_element_type=F32)
            grad = back.reshape(r2, COLS, CH) * (s * (1.0 + v * (1.0 - s)))
            store_wide(sw, at, keep_rows(grad, base - 2 + t * r2, height))
            part = jnp.dot((pack * mine).astype(BF16), act, preferred_element_type=F32)
            sums = [jnp.sum(d * mine, axis=1, keepdims=True) for d in dl]
            bias_row = jnp.where(
                lane[0:1] == 0, sums[0], jnp.where(lane[0:1] == 1, sums[1], jnp.where(lane[0:1] == 2, sums[2], 0.0))
            )
            small[0:3, :] += part[0:3] + part[3:6]
            small[3:4, :] += bias_row
            return c

        lax.fori_loop(0, n2, second, 0)

        def weight(grad_wide, skip, src, src_skip, out):
            gt[...] = grad_wide[skip * COLS:(skip + ROWS) * COLS, CH:2 * CH].T
            for a in range(3):
                win = src[(src_skip + a) * COLS:(src_skip + a + ROWS) * COLS, :]
                res = jnp.dot(gt[...], win, preferred_element_type=F32)
                for b in range(3):
                    out[(3 * a + b) * CH:(3 * a + b + 1) * CH, :] = (
                        res[:, b * CH:(b + 1) * CH].T.astype(BF16)
                    )

        weight(sw, 2, aw, 2, g2)

        def third(t, c):
            at = t * (rt * COLS)
            v = conv_rows(sw, at, rt, k2t)
            sl = slope[pl.ds(pl.multiple_of(at + 2 * COLS, COLS), rt * COLS), :]
            g = keep_rows(v * sl.reshape(rt, COLS, CH), base - 1 + t * rt, height)
            store_wide(fg, at, g)
            return c

        lax.fori_loop(0, nt, third, 0)
        weight(fg, 1, fw, 3, g1)

    return main


def main_call(band, f, k1, k2, k2t, cls, bias, lab, own, height, scale, **kw):
    vm = pl.BlockSpec(memory_space=pltpu.VMEM)
    return pl.pallas_call(
        make_main(height, scale, **kw),
        out_shape=(
            jax.ShapeDtypeStruct((9 * CH, CH), BF16),
            jax.ShapeDtypeStruct((9 * CH, CH), BF16),
            jax.ShapeDtypeStruct((8, CH), F32),
            jax.ShapeDtypeStruct((18 * COLS, 3 * CH), BF16),
        ),
        in_specs=[pl.BlockSpec(memory_space=pltpu.SMEM)] + [vm] * 8,
        out_specs=(vm,) * 4,
        scratch_shapes=[
            pltpu.VMEM((24 * COLS, 3 * CH), BF16),
            pltpu.VMEM((22 * COLS, 3 * CH), BF16),
            pltpu.VMEM((20 * COLS, 3 * CH), BF16),
            pltpu.VMEM((CH, ROWS * COLS), BF16),
            pltpu.VMEM((22 * COLS, CH), F32),
        ],
        compiler_params=pltpu.CompilerParams(vmem_limit_bytes=40 * 1024 * 1024),
        cost_estimate=pl.CostEstimate(flops=11_000_000_000, bytes_accessed=8_000_000, transcendentals=1_000_000),
        name="main",
    )(band, f, k1, k2, k2t, cls, bias, lab, own)


def feat_kernel(fg, k1t, out):
    def step(t, c):
        at = t * (4 * COLS)
        v = conv_rows(fg, at, 4, k1t)
        out[pl.ds(pl.multiple_of(at, COLS), 4 * COLS), :] = v.astype(BF16).reshape(4 * COLS, CH)
        return c

    lax.fori_loop(0, 4, step, 0)


def feat_call(fg, k1t):
    vm = pl.BlockSpec(memory_space=pltpu.VMEM)
    return pl.pallas_call(
        feat_kernel,
        out_shape=jax.ShapeDtypeStruct((ROWS * COLS, CH), BF16),
        in_specs=[vm] * 2,
        out_specs=vm,
        compiler_params=pltpu.CompilerParams(vmem_limit_bytes=16 * 1024 * 1024),
        cost_estimate=pl.CostEstimate(flops=1_800_000_000, bytes_accessed=4_000_000, transcendentals=0),
        name="feat",
    )(fg, k1t)


AXES = ("b", "x", "h", "y", "c")


def shift(value, axis, step, size):
    return lax.ppermute(value, axis, [(i, (i + step) % size) for i in range(size)])


def split_small(small):
    hi = small.astype(BF16)
    return jnp.concatenate([hi, (small - hi.astype(F32)).astype(BF16)], axis=0)


def join_small(rows):
    full = rows.astype(F32)
    return full[..., 0:8, :] + full[..., 8:16, :]


def per_device(features, first_kernel, second_kernel, classifier, class_bias, labels):
    height = ROWS * lax.axis_size("b")
    count = height * COLS * lax.axis_size("x") * lax.axis_size("h") * lax.axis_size("y") * lax.axis_size("c")
    scale = float(count) ** (-0.5)
    band = lax.axis_index("b")
    core = lax.axis_index("c")

    flat = features.reshape(ROWS * COLS, CH)
    lab = labels.reshape(ROWS * COLS)

    def edge(rows, tags):
        tag = jnp.pad(tags.astype(BF16), (0, 16 * CH - 2 * COLS)).reshape(16, CH)
        return jnp.concatenate([rows, tag], axis=0)

    down = [(i, i + 1) for i in range(3)]
    up = [(i + 1, i) for i in range(3)]
    above = lax.ppermute(edge(flat[12 * COLS:], lab[14 * COLS:]), "b", down)
    below = lax.ppermute(edge(flat[:4 * COLS], lab[:2 * COLS]), "b", up)
    ext = jnp.concatenate([above[:4 * COLS], flat, below[:4 * COLS]], axis=0)

    def tags(block):
        return block[4 * COLS:].reshape(-1)[:2 * COLS].astype(jnp.int32)

    lab_ext = jnp.concatenate([tags(above), lab, tags(below)]).reshape(5, 1, 4 * COLS)
    own = jnp.pad(jnp.ones((ROWS * COLS,), F32), (2 * COLS, 2 * COLS)).reshape(5, 1, 4 * COLS)
    cls = jnp.pad(jnp.concatenate([classifier.T, classifier.T], axis=0), ((0, 10), (0, 0)))
    bias = jnp.broadcast_to(jnp.pad(class_bias, (0, 5))[:, None], (8, 128))

    def flipped(kernel):
        return jnp.transpose(kernel[::-1, ::-1], (0, 1, 3, 2)).reshape(9 * CH, CH)

    g1, g2, small, fg = main_call(
        band.reshape(1), ext, first_kernel.reshape(9 * CH, CH), second_kernel.reshape(9 * CH, CH),
        flipped(second_kernel), cls, bias, lab_ext, own, height, scale, r1=11, rt=6,
    )
    grad_features = feat_call(fg, flipped(first_kernel)).reshape(features.shape)

    keep = jnp.where(core == 0, g1, g2)
    give = jnp.where(core == 0, g2, g1)
    got = shift(jnp.concatenate([give, split_small(small)], axis=0), "c", 1, 2)
    total = (keep.astype(F32) + got[:9 * CH].astype(F32)).astype(BF16)
    small = small + join_small(got[9 * CH:])

    part = 9 * CH // 16
    spread = jnp.concatenate(
        [total.reshape(16, part, CH), jnp.broadcast_to(split_small(small), (16, 16, CH))], axis=1
    )
    spread = lax.all_to_all(spread, ("x", "y"), 0, 0, tiled=True)
    piece = jnp.sum(spread[:, :part].astype(F32), axis=0).astype(BF16)
    small = jnp.sum(join_small(spread[:, part:]), axis=0)

    for axis, size in (("b", 4), ("h", 2)):
        send = jnp.concatenate([piece, split_small(small)], axis=0)
        others = [shift(send, axis, k, size) for k in range(1, size)]
        wide = piece.astype(F32)
        for other in others:
            wide = wide + other[:part].astype(F32)
            small = small + join_small(other[part:])
        piece = wide.astype(BF16)

    full = lax.all_to_all(jnp.broadcast_to(piece, (16, part, CH)), ("x", "y"), 0, 0, tiled=True)
    mine = full.reshape(9 * CH, CH)
    other = shift(mine, "c", 1, 2)
    grad_first = jnp.where(core == 0, mine, other).astype(F32).reshape(3, 3, CH, CH)
    grad_second = jnp.where(core == 0, other, mine).astype(F32).reshape(3, 3, CH, CH)
    return (grad_features, grad_first, grad_second, small[0:3].T, small[3, 0:3])


def solution(mesh):
    fine = Mesh(mesh.devices.reshape(4, 4, 2, 4, 2), AXES)
    rail = ("x", "h", "y", "c")
    placed = (P(rail, "b", None, None), P(), P(), P(), P(), P(rail, "b", None))
    return jax.shard_map(
        per_device,
        mesh=fine,
        in_specs=placed,
        out_specs=(P(rail, "b", None, None), P(), P(), P(), P()),
        check_vma=False,
    )
```

```python
import jax
import jax.numpy as jnp
from jax import lax
from jax.experimental import pallas as pl
from jax.experimental.pallas import tpu as pltpu
from jax.sharding import Mesh, PartitionSpec as P

ROWS = 16
COLS = 96
CH = 256
HALO = 4
PIX = ROWS * COLS
EDGE = HALO * COLS
BLOCK = EDGE + 16
F32 = jnp.float32
BF16 = jnp.bfloat16
ROWWISE = (((0,), (0,)), ((), ()))
VMEM = pl.BlockSpec(memory_space=pltpu.VMEM)
SMEM = pl.BlockSpec(memory_space=pltpu.SMEM)
AXES = ("b", "x", "h", "y", "c")


def call(kernel, outs, args, scratch=(), limit=24, flops=0, name=None, scalars=0, out_specs=None):
    moved = sum(a.size * a.dtype.itemsize for a in args)
    shapes = tuple(jax.ShapeDtypeStruct(s, d) for s, d in outs)
    return pl.pallas_call(
        kernel,
        out_shape=shapes,
        in_specs=[SMEM] * scalars + [VMEM] * (len(args) - scalars),
        out_specs=(VMEM,) * len(outs) if out_specs is None else out_specs,
        scratch_shapes=list(scratch),
        compiler_params=pltpu.CompilerParams(vmem_limit_bytes=limit * 1024 * 1024),
        cost_estimate=pl.CostEstimate(flops=flops, bytes_accessed=moved, transcendentals=0),
        name=name,
    )(*args)


def conv_rows(wide, start, count, kernel):
    patch = jnp.concatenate(
        [wide[pl.ds(pl.multiple_of(start + a * COLS, COLS), count * COLS), :] for a in range(3)],
        axis=1,
    )
    out = jnp.dot(patch, kernel[...], preferred_element_type=F32)
    return out.reshape(count, COLS, CH)


def store_wide(wide, start, rows):
    count = rows.shape[0]
    col = lax.broadcasted_iota(jnp.int32, rows.shape, 1)
    left = jnp.where(col == 0, 0.0, pltpu.roll(rows, 1, 1))
    right = jnp.where(col == COLS - 1, 0.0, pltpu.roll(rows, COLS - 1, 1))
    at = pl.ds(pl.multiple_of(start, COLS), count * COLS)
    wide[at, 0:CH] = left.astype(BF16).reshape(count * COLS, CH)
    wide[at, CH:2 * CH] = rows.astype(BF16).reshape(count * COLS, CH)
    wide[at, 2 * CH:3 * CH] = right.astype(BF16).reshape(count * COLS, CH)


def load_rows(ref, start, count):
    at = pl.ds(pl.multiple_of(start, COLS), count * COLS)
    return ref[at, :].astype(F32).reshape(count, COLS, CH)


def sigmoid(value):
    return 0.5 * jnp.tanh(0.5 * value) + 0.5


def keep_rows(rows, first, height):
    parts = []
    for r in range(rows.shape[0]):
        inside = jnp.logical_and(first + r >= 0, first + r < height)
        parts.append(rows[r] * jnp.where(inside, 1.0, 0.0))
    return jnp.stack(parts)


def edge_kernel(f, lab, up, down, tag):
    for out, row, label in ((up, 0, 0), (down, ROWS - HALO, ROWS - 2)):
        out[0:EDGE, :] = f[row * COLS:(row + HALO) * COLS, :]
        tag[...] = jnp.zeros_like(tag)
        tag[0:2, 0:COLS] = lab[label:label + 2, :].astype(F32)
        out[EDGE:BLOCK, :] = tag[...].astype(BF16)


def inner_kernel(f, k1, k2, fw, aw, slope, k1t, k2t):
    def widen(t, c):
        store_wide(fw, t * (2 * COLS), load_rows(f, t * (2 * COLS), 2))
        return c

    lax.fori_loop(0, 8, widen, 0)

    def first(t, c):
        at = t * (7 * COLS)
        v = conv_rows(fw, at, 7, k1)
        s = sigmoid(v)
        rows = pl.ds(pl.multiple_of(at, COLS), 7 * COLS)
        slope[rows, :] = (s * (1.0 + v * (1.0 - s))).reshape(7 * COLS, CH)
        store_wide(aw, at, v * s)
        return c

    lax.fori_loop(0, 2, first, 0)

    for t in range(9):
        for src, dst in ((k1, k1t), (k2, k2t)):
            dst[t * CH:(t + 1) * CH, :] = src[(8 - t) * CH:(9 - t) * CH, :].T


def make_main(height, scale):
    def main(ids, above, below, fwi, awi, slopei, k1, k2, k2t, cls, bias, lab, g1, g2, small, fg,
             fw, aw, sw, fgw, gt, slope, labs):
        base = ids[0] * ROWS
        fw[EDGE:EDGE + PIX, :] = fwi[...]
        for half in range(2):
            at = half * 2 * COLS
            rows = keep_rows(load_rows(above, at, 2), base - HALO + half * 2, height)
            store_wide(fw, at, rows)
            rows = keep_rows(load_rows(below, at, 2), base + ROWS + half * 2, height)
            store_wide(fw, EDGE + PIX + at, rows)
        aw[4 * COLS:18 * COLS, :] = awi[...]
        slope[4 * COLS:18 * COLS, :] = slopei[...]

        tags = [above[EDGE:BLOCK, :].astype(F32), below[EDGE:BLOCK, :].astype(F32)]
        mine = lab[...].astype(F32)
        lines = [tags[0][0:1, 0:COLS], tags[0][1:2, 0:COLS]]
        lines += [mine[r:r + 1, :] for r in range(ROWS)]
        lines += [tags[1][0:1, 0:COLS], tags[1][1:2, 0:COLS]]
        for r, line in enumerate(lines):
            labs[r // 10, 0:1, (r % 10) * COLS:(r % 10 + 1) * COLS] = line

        def first(t, c):
            at = t * (18 * COLS)
            v = conv_rows(fw, at, 4, k1)
            s = sigmoid(v)
            rows = pl.ds(pl.multiple_of(at, COLS), 4 * COLS)
            slope[rows, :] = (s * (1.0 + v * (1.0 - s))).reshape(4 * COLS, CH)
            store_wide(aw, at, keep_rows(v * s, base - 3 + t * 18, height))
            return c

        lax.fori_loop(0, 2, first, 0)

        small[...] = jnp.zeros_like(small)
        lane = lax.broadcasted_iota(jnp.int32, (1, CH), 1)
        pixel = lax.broadcasted_iota(jnp.int32, (1, 10 * COLS), 1)

        def second(t, c):
            at = t * (10 * COLS)
            v = conv_rows(aw, at, 10, k2)
            s = sigmoid(v)
            act = (v * s).astype(BF16).reshape(10 * COLS, CH)
            logit = lax.dot_general(
                cls[...], act, (((1,), (1,)), ((), ())), preferred_element_type=F32
            )
            rows = [logit[k:k + 1, :] + bias[k:k + 1, 0:1] for k in range(3)]
            top = jnp.maximum(jnp.maximum(rows[0], rows[1]), rows[2])
            ex = [jnp.exp(row - top) for row in rows]
            den = ex[0] + ex[1] + ex[2]
            label = labs[t][0:1, 0:10 * COLS]
            place = pixel + at
            own = jnp.where(jnp.logical_and(place >= 2 * COLS, place < 18 * COLS), 1.0, 0.0)
            dl = [(ex[k] / den - jnp.where(label == k, 1.0, 0.0)) * scale for k in range(3)]
            hi = [d.astype(BF16).astype(F32) for d in dl]
            lo = [d - h for d, h in zip(dl, hi)]
            zero = jnp.zeros((10, 10 * COLS), F32)
            pack = jnp.concatenate(hi + lo + [zero], axis=0)
            back = lax.dot_general(pack.astype(BF16), cls[...], ROWWISE, preferred_element_type=F32)
            grad = back.reshape(10, COLS, CH) * (s * (1.0 + v * (1.0 - s)))
            store_wide(sw, at, keep_rows(grad, base - 2 + t * 10, height))
            part = jnp.dot((pack * own).astype(BF16), act, preferred_element_type=F32)
            sums = [jnp.sum(d * own, axis=1, keepdims=True) for d in dl]
            row = jnp.where(lane == 0, sums[0], jnp.where(lane == 1, sums[1], 0.0))
            small[0:3, :] += part[0:3] + part[3:6]
            small[3:4, :] += jnp.where(lane == 2, sums[2], row)
            return c

        lax.fori_loop(0, 2, second, 0)

        def weight(grad_wide, skip, src, src_skip, out):
            gt[...] = grad_wide[skip * COLS:(skip + ROWS) * COLS, CH:2 * CH].T
            for a in range(3):
                win = src[(src_skip + a) * COLS:(src_skip + a + ROWS) * COLS, :]
                res = jnp.dot(gt[...], win, preferred_element_type=F32)
                for b in range(3):
                    out[(3 * a + b) * CH:(3 * a + b + 1) * CH, :] = (
                        res[:, b * CH:(b + 1) * CH].T.astype(BF16)
                    )

        weight(sw, 2, aw, 2, g2)

        def third(t, c):
            at = t * (6 * COLS)
            v = conv_rows(sw, at, 6, k2t)
            sl = slope[pl.ds(pl.multiple_of(at + 2 * COLS, COLS), 6 * COLS), :]
            g = keep_rows(v * sl.reshape(6, COLS, CH), base - 1 + t * 6, height)
            store_wide(fgw, at, g)
            return c

        lax.fori_loop(0, 3, third, 0)
        weight(fgw, 1, fw, 3, g1)
        fg[...] = fgw[:, CH:2 * CH]

    return main


def feature_kernel(fg, k1t, out, fgw):
    def widen(t, c):
        store_wide(fgw, t * (2 * COLS), load_rows(fg, t * (2 * COLS), 2))
        return c

    lax.fori_loop(0, 9, widen, 0)

    def step(t, c):
        at = t * (8 * COLS)
        v = conv_rows(fgw, at, 8, k1t)
        out[pl.ds(pl.multiple_of(at, COLS), 8 * COLS), :] = v.astype(BF16).reshape(8 * COLS, CH)
        return c

    lax.fori_loop(0, 2, step, 0)


def final_kernel(ids, mine, other, g1, g2, wide, sems):
    copies = []
    for t in range(3):
        at = pl.ds(t * 768, 768)
        for k, block in enumerate((mine, other)):
            wide[k, at, :] = block[at, :].astype(F32)
        for k, out in enumerate((g1, g2)):
            slot = ids[1] if k == 0 else 1 - ids[1]
            copy = pltpu.make_async_copy(wide.at[slot, at], out.at[at], sems.at[k, t])
            copy.start()
            copies.append(copy)
    for copy in copies:
        copy.wait()


def ring(step):
    def place(z):
        return (z % 4) * 2 + z // 4

    return [(place(z), place((z + step) % 8)) for z in range(8)]


def shift(value, axis, step, size):
    return lax.ppermute(value, axis, [(i, (i + step) % size) for i in range(size)])


def split_small(small):
    hi = small.astype(BF16)
    return jnp.concatenate([hi, (small - hi.astype(F32)).astype(BF16)], axis=0)


def join_small(rows):
    full = rows.astype(F32)
    return full[..., 0:8, :] + full[..., 8:16, :]


def per_device(features, first_kernel, second_kernel, classifier, class_bias, labels):
    height = ROWS * lax.axis_size("b")
    count = height * COLS * lax.axis_size("x") * lax.axis_size("h") * lax.axis_size("y") * lax.axis_size("c")
    scale = float(count) ** (-0.5)
    band = lax.axis_index("b")
    core = lax.axis_index("c")
    ids = jnp.stack([band, core])

    flat = features.reshape(PIX, CH)
    lab = labels.reshape(ROWS, COLS)
    k1 = first_kernel.reshape(9 * CH, CH)
    k2 = second_kernel.reshape(9 * CH, CH)
    up, down = call(
        edge_kernel, [((BLOCK, CH), BF16)] * 2, (flat, lab),
        [pltpu.VMEM((16, CH), F32)], limit=8, name="edge",
    )
    above = lax.ppermute(down, ("b", "h"), ring(1))
    below = lax.ppermute(up, ("b", "h"), ring(7))

    fwi, awi, slopei, k1t, k2t = call(
        inner_kernel,
        [((PIX, 3 * CH), BF16), ((14 * COLS, 3 * CH), BF16), ((14 * COLS, CH), F32),
         ((9 * CH, CH), BF16), ((9 * CH, CH), BF16)],
        (flat, k1, k2), flops=5_000_000_000, name="inner",
    )

    cls = jnp.pad(jnp.concatenate([classifier.T, classifier.T], axis=0), ((0, 10), (0, 0)))
    bias = jnp.broadcast_to(jnp.pad(class_bias, (0, 5))[:, None], (8, 128))
    g1, g2, small, fg = call(
        make_main(height, scale),
        [((9 * CH, CH), BF16), ((9 * CH, CH), BF16), ((8, CH), F32), ((18 * COLS, CH), BF16)],
        (ids, above, below, fwi, awi, slopei, k1, k2, k2t, cls, bias, lab),
        [
            pltpu.VMEM((24 * COLS, 3 * CH), BF16),
            pltpu.VMEM((22 * COLS, 3 * CH), BF16),
            pltpu.VMEM((20 * COLS, 3 * CH), BF16),
            pltpu.VMEM((18 * COLS, 3 * CH), BF16),
            pltpu.VMEM((CH, PIX), BF16),
            pltpu.VMEM((22 * COLS, CH), F32),
            pltpu.VMEM((2, 8, 1024), F32),
        ],
        limit=40, flops=9_000_000_000, name="main", scalars=1,
    )
    (grad_features,) = call(
        feature_kernel, [((PIX, CH), BF16)], (fg, k1t),
        [pltpu.VMEM((18 * COLS, 3 * CH), BF16)], limit=16, flops=2_500_000_000, name="feature",
    )

    keep = jnp.where(core == 0, g1, g2)
    give = jnp.where(core == 0, g2, g1)
    got = shift(jnp.concatenate([give, split_small(small)], axis=0), "c", 1, 2)
    total = (keep.astype(F32) + got[:9 * CH].astype(F32)).astype(BF16)
    small = small + join_small(got[9 * CH:])

    part = 9 * CH // 16
    spread = jnp.concatenate(
        [total.reshape(16, part, CH), jnp.broadcast_to(split_small(small), (16, 16, CH))], axis=1
    )
    spread = lax.all_to_all(spread, ("x", "y"), 0, 0, tiled=True)
    piece = jnp.sum(spread[:, :part].astype(F32), axis=0).astype(BF16)
    small = jnp.sum(join_small(spread[:, part:]), axis=0)

    pair = [(0, 1), (1, 0), (2, 3), (3, 2)]
    for moves in ((("b", pair),), tuple((("b", "h"), ring(k)) for k in (2, 6, 4))):
        send = jnp.concatenate([piece, split_small(small)], axis=0)
        others = [lax.ppermute(send, axis, move) for axis, move in moves]
        wide = piece.astype(F32)
        for other in others:
            wide = wide + other[:part].astype(F32)
            small = small + join_small(other[part:])
        piece = wide.astype(BF16)

    full = lax.all_to_all(jnp.broadcast_to(piece, (16, part, CH)), ("x", "y"), 0, 0, tiled=True)
    mine = full.reshape(9 * CH, CH)
    other = shift(mine, "c", 1, 2)
    hbm = pl.BlockSpec(memory_space=pl.ANY)
    grad_first, grad_second = call(
        final_kernel, [((9 * CH, CH), F32)] * 2, (ids, mine, other),
        [pltpu.VMEM((2, 9 * CH, CH), F32), pltpu.SemaphoreType.DMA((2, 3))],
        limit=16, name="final", scalars=1, out_specs=(hbm, hbm),
    )
    shape = (3, 3, CH, CH)
    return (
        grad_features.reshape(features.shape), grad_first.reshape(shape), grad_second.reshape(shape),
        small[0:3].T, small[3, 0:3],
    )


def solution(mesh):
    fine = Mesh(mesh.devices.reshape(4, 4, 2, 4, 2), AXES)
    rail = ("x", "h", "y", "c")
    placed = (P(rail, "b", None, None), P(), P(), P(), P(), P(rail, "b", None))
    return jax.shard_map(
        per_device,
        mesh=fine,
        in_specs=placed,
        out_specs=(P(rail, "b", None, None), P(), P(), P(), P()),
        check_vma=False,
    )
```

```python
import jax
import jax.numpy as jnp
from jax import lax
from jax.experimental import pallas as pl
from jax.experimental.pallas import tpu as pltpu
from jax.sharding import Mesh, PartitionSpec as P

ROWS = 16
COLS = 96
CH = 256
HALO = 4
PIX = ROWS * COLS
EDGE = HALO * COLS
BLOCK = EDGE + 16
F32 = jnp.float32
BF16 = jnp.bfloat16
ROWWISE = (((0,), (0,)), ((), ()))
VMEM = pl.BlockSpec(memory_space=pltpu.VMEM)
SMEM = pl.BlockSpec(memory_space=pltpu.SMEM)
HBM = pl.BlockSpec(memory_space=pltpu.HBM)
AXES = ("b", "x", "h", "y", "c")


def call(kernel, outs, args, ins, scratch=(), limit=24, flops=0, name=None, out_specs=None, aliases={}):
    moved = sum(a.size * a.dtype.itemsize for a in args)
    shapes = tuple(jax.ShapeDtypeStruct(s, d) for s, d in outs)
    return pl.pallas_call(
        kernel,
        out_shape=shapes,
        in_specs=list(ins),
        input_output_aliases=aliases,
        out_specs=(VMEM,) * len(outs) if out_specs is None else out_specs,
        scratch_shapes=list(scratch),
        compiler_params=pltpu.CompilerParams(vmem_limit_bytes=limit * 1024 * 1024),
        cost_estimate=pl.CostEstimate(flops=flops, bytes_accessed=moved, transcendentals=0),
        name=name,
    )(*args)


def aligned(start):
    return start if isinstance(start, int) else pl.multiple_of(start, COLS)


def conv_rows(wide, start, count, kernel):
    patch = jnp.concatenate(
        [wide[pl.ds(aligned(start + a * COLS), count * COLS), :] for a in range(3)], axis=1
    )
    out = jnp.dot(patch, kernel[...], preferred_element_type=F32)
    return out.reshape(count, COLS, CH)


def store_wide(wide, start, rows):
    count = rows.shape[0]
    col = lax.broadcasted_iota(jnp.int32, rows.shape, 1)
    left = jnp.where(col == 0, 0.0, pltpu.roll(rows, 1, 1))
    right = jnp.where(col == COLS - 1, 0.0, pltpu.roll(rows, COLS - 1, 1))
    at = pl.ds(aligned(start), count * COLS)
    wide[at, 0:CH] = left.astype(BF16).reshape(count * COLS, CH)
    wide[at, CH:2 * CH] = rows.astype(BF16).reshape(count * COLS, CH)
    wide[at, 2 * CH:3 * CH] = right.astype(BF16).reshape(count * COLS, CH)


def load_rows(ref, start, count):
    at = pl.ds(aligned(start), count * COLS)
    return ref[at, :].astype(F32).reshape(count, COLS, CH)


def sigmoid(value):
    return 0.5 * jnp.tanh(0.5 * value) + 0.5


def keep_rows(rows, first, height):
    parts = []
    for r in range(rows.shape[0]):
        inside = jnp.logical_and(first + r >= 0, first + r < height)
        parts.append(rows[r] * jnp.where(inside, 1.0, 0.0))
    return jnp.stack(parts)


def edge_kernel(f, lab, up, down, fv, labels, tag):
    for out, row, label in ((up, 0, 0), (down, ROWS - HALO, ROWS - 2)):
        out[0:EDGE, :] = f[row * COLS:(row + HALO) * COLS, :]
        tag[...] = jnp.zeros_like(tag)
        tag[0:2, 0:COLS] = lab[label:label + 2, :].astype(F32)
        out[EDGE:BLOCK, :] = tag[...].astype(BF16)
    fv[...] = f[...]
    labels[...] = lab[...]


def inner_kernel(f, k1, k2, fw, aw, slope, k1t, k2t):
    def widen(t, c):
        store_wide(fw, t * (2 * COLS), load_rows(f, t * (2 * COLS), 2))
        return c

    lax.fori_loop(0, 8, widen, 0)

    for t in range(7):
        at = t * (2 * COLS)
        v = conv_rows(fw, at, 2, k1)
        s = sigmoid(v)
        slope[pl.ds(at, 2 * COLS), :] = (s * (1.0 + v * (1.0 - s))).reshape(2 * COLS, CH)
        store_wide(aw, at, v * s)

    for t in range(9):
        for src, dst in ((k1, k1t), (k2, k2t)):
            dst[t * CH:(t + 1) * CH, :] = src[(8 - t) * CH:(9 - t) * CH, :].T


def make_main(height, scale):
    def main(ids, above, below, fwi, awi, slopei, k1, k2, k2t, cls, bias, lab, g1, g2, small, fg,
             fw, aw, sw, fgw, gt, slope, labs):
        base = ids[0] * ROWS
        fw[EDGE:EDGE + PIX, :] = fwi[...]
        for half in range(2):
            at = half * 2 * COLS
            rows = keep_rows(load_rows(above, at, 2), base - HALO + half * 2, height)
            store_wide(fw, at, rows)
            rows = keep_rows(load_rows(below, at, 2), base + ROWS + half * 2, height)
            store_wide(fw, EDGE + PIX + at, rows)
        aw[4 * COLS:18 * COLS, :] = awi[...]
        slope[4 * COLS:18 * COLS, :] = slopei[...]

        tags = [above[EDGE:BLOCK, :].astype(F32), below[EDGE:BLOCK, :].astype(F32)]
        mine = lab[...].astype(F32)
        lines = [tags[0][0:1, 0:COLS], tags[0][1:2, 0:COLS]]
        lines += [mine[r:r + 1, :] for r in range(ROWS)]
        lines += [tags[1][0:1, 0:COLS], tags[1][1:2, 0:COLS]]
        for r, line in enumerate(lines):
            labs[r // 10, 0:1, (r % 10) * COLS:(r % 10 + 1) * COLS] = line

        def first(t, c):
            at = t * (18 * COLS)
            v = conv_rows(fw, at, 4, k1)
            s = sigmoid(v)
            rows = pl.ds(aligned(at), 4 * COLS)
            slope[rows, :] = (s * (1.0 + v * (1.0 - s))).reshape(4 * COLS, CH)
            store_wide(aw, at, keep_rows(v * s, base - 3 + t * 18, height))
            return c

        lax.fori_loop(0, 2, first, 0)

        small[...] = jnp.zeros_like(small)
        lane = lax.broadcasted_iota(jnp.int32, (1, CH), 1)
        pixel = lax.broadcasted_iota(jnp.int32, (1, 10 * COLS), 1)

        def second(t, c):
            at = t * (10 * COLS)
            v = conv_rows(aw, at, 10, k2)
            s = sigmoid(v)
            act = (v * s).astype(BF16).reshape(10 * COLS, CH)
            logit = lax.dot_general(
                cls[...], act, (((1,), (1,)), ((), ())), preferred_element_type=F32
            )
            rows = [logit[k:k + 1, :] + bias[k:k + 1, 0:1] for k in range(3)]
            top = jnp.maximum(jnp.maximum(rows[0], rows[1]), rows[2])
            ex = [jnp.exp(row - top) for row in rows]
            den = ex[0] + ex[1] + ex[2]
            label = labs[t][0:1, 0:10 * COLS]
            place = pixel + at
            own = jnp.where(jnp.logical_and(place >= 2 * COLS, place < 18 * COLS), 1.0, 0.0)
            dl = [(ex[k] / den - jnp.where(label == k, 1.0, 0.0)) * scale for k in range(3)]
            hi = [d.astype(BF16).astype(F32) for d in dl]
            lo = [d - h for d, h in zip(dl, hi)]
            zero = jnp.zeros((10, 10 * COLS), F32)
            pack = jnp.concatenate(hi + lo + [zero], axis=0)
            back = lax.dot_general(pack.astype(BF16), cls[...], ROWWISE, preferred_element_type=F32)
            grad = back.reshape(10, COLS, CH) * (s * (1.0 + v * (1.0 - s)))
            store_wide(sw, at, keep_rows(grad, base - 2 + t * 10, height))
            part = jnp.dot((pack * own).astype(BF16), act, preferred_element_type=F32)
            sums = [jnp.sum(d * own, axis=1, keepdims=True) for d in dl]
            row = jnp.where(lane == 0, sums[0], jnp.where(lane == 1, sums[1], 0.0))
            small[0:3, :] += part[0:3] + part[3:6]
            small[3:4, :] += jnp.where(lane == 2, sums[2], row)
            return c

        lax.fori_loop(0, 2, second, 0)

        def weight(grad_wide, skip, src, src_skip, out):
            gt[...] = grad_wide[skip * COLS:(skip + ROWS) * COLS, CH:2 * CH].T
            for a in range(3):
                win = src[(src_skip + a) * COLS:(src_skip + a + ROWS) * COLS, :]
                res = jnp.dot(gt[...], win, preferred_element_type=F32)
                for b in range(3):
                    out[(3 * a + b) * CH:(3 * a + b + 1) * CH, :] = (
                        res[:, b * CH:(b + 1) * CH].T.astype(BF16)
                    )

        weight(sw, 2, aw, 2, g2)

        for t in range(6):
            at = t * (3 * COLS)
            v = conv_rows(sw, at, 3, k2t)
            sl = slope[pl.ds(at + 2 * COLS, 3 * COLS), :]
            g = keep_rows(v * sl.reshape(3, COLS, CH), base - 1 + t * 3, height)
            store_wide(fgw, at, g)
        weight(fgw, 1, fw, 3, g1)
        fg[...] = fgw[:, CH:2 * CH]

    return main


def feature_kernel(fg, k1t, out, fgw):
    def widen(t, c):
        store_wide(fgw, t * (2 * COLS), load_rows(fg, t * (2 * COLS), 2))
        return c

    lax.fori_loop(0, 9, widen, 0)

    def step(t, c):
        at = t * (8 * COLS)
        v = conv_rows(fgw, at, 8, k1t)
        out[pl.ds(aligned(at), 8 * COLS), :] = v.astype(BF16).reshape(8 * COLS, CH)
        return c

    lax.fori_loop(0, 2, step, 0)


def convert_out(block, wide, out, sems):
    copies = []
    for t in range(3):
        at = pl.ds(t * 768, 768)
        wide[at, :] = block[at, :].astype(F32)
        copies.append(pltpu.make_async_copy(wide.at[at], out.at[at], sems.at[t]))
        copies[-1].start()
    for copy in copies:
        copy.wait()


def mine_kernel(ids, mine, g1, g2, wide, sems):
    @pl.when(ids[1] == 0)
    def _():
        convert_out(mine, wide, g1, sems)

    @pl.when(ids[1] == 1)
    def _():
        convert_out(mine, wide, g2, sems)


def other_kernel(ids, other, g1_in, g2_in, g1, g2, wide, sems):
    mine_kernel(ids, other, g2, g1, wide, sems)


def ring(step):
    def place(z):
        return (z % 4) * 2 + z // 4

    return [(place(z), place((z + step) % 8)) for z in range(8)]


def shift(value, axis, step, size):
    return lax.ppermute(value, axis, [(i, (i + step) % size) for i in range(size)])


def split_small(small):
    hi = small.astype(BF16)
    return jnp.concatenate([hi, (small - hi.astype(F32)).astype(BF16)], axis=0)


def join_small(rows):
    full = rows.astype(F32)
    return full[..., 0:4, :] + full[..., 4:8, :]


def per_device(features, first_kernel, second_kernel, classifier, class_bias, labels):
    height = ROWS * lax.axis_size("b")
    count = height * COLS * lax.axis_size("x") * lax.axis_size("h") * lax.axis_size("y") * lax.axis_size("c")
    scale = float(count) ** (-0.5)
    band = lax.axis_index("b")
    core = lax.axis_index("c")
    ids = jnp.stack([band, core])

    flat = features.reshape(PIX, CH)
    lab = labels.reshape(ROWS, COLS)
    k1 = first_kernel.reshape(9 * CH, CH)
    k2 = second_kernel.reshape(9 * CH, CH)
    up, down, fv, labels = call(
        edge_kernel,
        [((BLOCK, CH), BF16), ((BLOCK, CH), BF16), ((PIX, CH), BF16), ((ROWS, COLS), jnp.int32)],
        (flat, lab), [VMEM] * 2, [pltpu.VMEM((16, CH), F32)], limit=8, name="edge",
    )
    above = lax.ppermute(down, ("b", "h"), ring(1))
    below = lax.ppermute(up, ("b", "h"), ring(7))

    fwi, awi, slopei, k1t, k2t = call(
        inner_kernel,
        [((PIX, 3 * CH), BF16), ((14 * COLS, 3 * CH), BF16), ((14 * COLS, CH), F32),
         ((9 * CH, CH), BF16), ((9 * CH, CH), BF16)],
        (fv, k1, k2), [VMEM] * 3,
        flops=5_000_000_000, name="inner",
    )

    cls = jnp.pad(jnp.concatenate([classifier.T, classifier.T], axis=0), ((0, 10), (0, 0)))
    bias = jnp.broadcast_to(jnp.pad(class_bias, (0, 5))[:, None], (8, 128))
    g1, g2, small, fg = call(
        make_main(height, scale),
        [((9 * CH, CH), BF16), ((9 * CH, CH), BF16), ((8, CH), F32), ((18 * COLS, CH), BF16)],
        (ids, above, below, fwi, awi, slopei, k1, k2, k2t, cls, bias, labels), [SMEM] + [VMEM] * 11,
        [
            pltpu.VMEM((24 * COLS, 3 * CH), BF16),
            pltpu.VMEM((22 * COLS, 3 * CH), BF16),
            pltpu.VMEM((20 * COLS, 3 * CH), BF16),
            pltpu.VMEM((18 * COLS, 3 * CH), BF16),
            pltpu.VMEM((CH, PIX), BF16),
            pltpu.VMEM((22 * COLS, CH), F32),
            pltpu.VMEM((2, 8, 1024), F32),
        ],
        limit=40, flops=9_000_000_000, name="main",
    )
    (grad_features,) = call(
        feature_kernel, [((PIX, CH), BF16)], (fg, k1t), [VMEM] * 2,
        [pltpu.VMEM((18 * COLS, 3 * CH), BF16)], limit=16, flops=2_500_000_000, name="feature",
    )

    small = small[0:4]
    keep = jnp.where(core == 0, g1, g2)
    give = jnp.where(core == 0, g2, g1)
    got = shift(jnp.concatenate([give, split_small(small)], axis=0), "c", 1, 2)
    total = (keep.astype(F32) + got[:9 * CH].astype(F32)).astype(BF16)
    small = small + join_small(got[9 * CH:])

    part = 9 * CH // 16
    spread = jnp.concatenate(
        [total.reshape(16, part, CH), jnp.broadcast_to(split_small(small), (16, 8, CH))], axis=1
    )
    spread = lax.all_to_all(spread, ("x", "y"), 0, 0, tiled=True)
    piece = jnp.sum(spread[:, :part].astype(F32), axis=0).astype(BF16)
    small = jnp.sum(join_small(spread[:, part:]), axis=0)

    pair = [(0, 1), (1, 0), (2, 3), (3, 2)]
    for moves in ((("b", pair),), tuple((("b", "h"), ring(k)) for k in (2, 6, 4))):
        send = jnp.concatenate([piece, split_small(small)], axis=0)
        others = [lax.ppermute(send, axis, move) for axis, move in moves]
        wide = piece.astype(F32)
        for other in others:
            wide = wide + other[:part].astype(F32)
            small = small + join_small(other[part:])
        piece = wide.astype(BF16)

    full = lax.all_to_all(jnp.broadcast_to(piece, (16, part, CH)), ("x", "y"), 0, 0, tiled=True)
    mine = full.reshape(9 * CH, CH)
    other = shift(mine, "c", 1, 2)
    outs = [((9 * CH, CH), F32)] * 2
    scratch = [pltpu.VMEM((9 * CH, CH), F32), pltpu.SemaphoreType.DMA((3,))]
    halves = call(
        mine_kernel, outs, (ids, mine), [SMEM, VMEM], scratch,
        limit=8, flops=1_000_000_000, name="mine", out_specs=(HBM, HBM),
    )
    grad_first, grad_second = call(
        other_kernel, outs, (ids, other, *halves), [SMEM, VMEM, HBM, HBM], scratch,
        limit=8, name="other", out_specs=(HBM, HBM), aliases={2: 0, 3: 1},
    )
    shape = (3, 3, CH, CH)
    return (
        grad_features.reshape(features.shape), grad_first.reshape(shape), grad_second.reshape(shape),
        small[0:3].T, small[3, 0:3],
    )


def solution(mesh):
    fine = Mesh(mesh.devices.reshape(4, 4, 2, 4, 2), AXES)
    rail = ("x", "h", "y", "c")
    placed = (P(rail, "b", None, None), P(), P(), P(), P(), P(rail, "b", None))
    return jax.shard_map(
        per_device,
        mesh=fine,
        in_specs=placed,
        out_specs=(P(rail, "b", None, None), P(), P(), P(), P()),
        check_vma=False,
    )
```

```python
import jax
import jax.numpy as jnp
from jax import lax
from jax.experimental import pallas as pl
from jax.experimental.pallas import tpu as pltpu
from jax.sharding import Mesh, PartitionSpec as P

ROWS = 16
COLS = 96
CH = 256
HALO = 4
PIX = ROWS * COLS
EDGE = HALO * COLS
BLOCK = EDGE + 16
F32 = jnp.float32
BF16 = jnp.bfloat16
ROWWISE = (((0,), (0,)), ((), ()))
VMEM = pl.BlockSpec(memory_space=pltpu.VMEM)
SMEM = pl.BlockSpec(memory_space=pltpu.SMEM)
HBM = pl.BlockSpec(memory_space=pltpu.HBM)
AXES = ("q", "p", "x", "h", "y", "c")
BAND = ("q", "p")
DEPTH = ("q", "p", "h")
PLANE = ("p", "x", "y")
RAIL = ("x", "h", "y", "c")


def call(kernel, outs, args, ins, scratch=(), limit=24, flops=0, name=None, out_specs=None, aliases={}):
    moved = sum(a.size * a.dtype.itemsize for a in args)
    shapes = tuple(jax.ShapeDtypeStruct(s, d) for s, d in outs)
    return pl.pallas_call(
        kernel,
        out_shape=shapes,
        in_specs=list(ins),
        input_output_aliases=aliases,
        out_specs=(VMEM,) * len(outs) if out_specs is None else out_specs,
        scratch_shapes=list(scratch),
        compiler_params=pltpu.CompilerParams(vmem_limit_bytes=limit * 1024 * 1024),
        cost_estimate=pl.CostEstimate(flops=flops, bytes_accessed=moved, transcendentals=0),
        name=name,
    )(*args)


def aligned(start):
    return start if isinstance(start, int) else pl.multiple_of(start, COLS)


def conv_rows(wide, start, count, kernel):
    patch = jnp.concatenate(
        [wide[pl.ds(aligned(start + a * COLS), count * COLS), :] for a in range(3)], axis=1
    )
    out = jnp.dot(patch, kernel[...], preferred_element_type=F32)
    return out.reshape(count, COLS, CH)


def store_wide(wide, start, rows):
    count = rows.shape[0]
    col = lax.broadcasted_iota(jnp.int32, rows.shape, 1)
    left = jnp.where(col == 0, 0.0, pltpu.roll(rows, 1, 1))
    right = jnp.where(col == COLS - 1, 0.0, pltpu.roll(rows, COLS - 1, 1))
    at = pl.ds(aligned(start), count * COLS)
    wide[at, 0:CH] = left.astype(BF16).reshape(count * COLS, CH)
    wide[at, CH:2 * CH] = rows.astype(BF16).reshape(count * COLS, CH)
    wide[at, 2 * CH:3 * CH] = right.astype(BF16).reshape(count * COLS, CH)


def load_rows(ref, start, count):
    at = pl.ds(aligned(start), count * COLS)
    return ref[at, :].astype(F32).reshape(count, COLS, CH)


def sigmoid(value):
    return 0.5 * jnp.tanh(0.5 * value) + 0.5


def keep_rows(rows, first, height):
    parts = []
    for r in range(rows.shape[0]):
        inside = jnp.logical_and(first + r >= 0, first + r < height)
        parts.append(rows[r] * jnp.where(inside, 1.0, 0.0))
    return jnp.stack(parts)


def edge_kernel(f, lab, up, down, fv, labels, tag):
    for out, row, label in ((up, 0, 0), (down, ROWS - HALO, ROWS - 2)):
        out[0:EDGE, :] = f[row * COLS:(row + HALO) * COLS, :]
        tag[...] = jnp.zeros_like(tag)
        tag[0:2, 0:COLS] = lab[label:label + 2, :].astype(F32)
        out[EDGE:BLOCK, :] = tag[...].astype(BF16)
    fv[...] = f[...]
    labels[...] = lab[...]


def inner_kernel(f, k1, k2, fw, aw, slope, k1t, k2t):
    def widen(t, c):
        store_wide(fw, t * (2 * COLS), load_rows(f, t * (2 * COLS), 2))
        return c

    lax.fori_loop(0, 8, widen, 0)

    for t in range(7):
        at = t * (2 * COLS)
        v = conv_rows(fw, at, 2, k1)
        s = sigmoid(v)
        slope[pl.ds(at, 2 * COLS), :] = (s * (1.0 + v * (1.0 - s))).reshape(2 * COLS, CH)
        store_wide(aw, at, v * s)

    for t in range(9):
        for src, dst in ((k1, k1t), (k2, k2t)):
            dst[t * CH:(t + 1) * CH, :] = src[(8 - t) * CH:(9 - t) * CH, :].T


def make_main(height, scale):
    def main(ids, above, below, fwi, awi, slopei, k1, k2, k2t, cls, bias, lab, g1, g2, small, fg,
             fw, aw, sw, fgw, gt, slope, labs):
        base = ids[0] * ROWS
        fw[EDGE:EDGE + PIX, :] = fwi[...]
        for half in range(2):
            at = half * 2 * COLS
            rows = keep_rows(load_rows(above, at, 2), base - HALO + half * 2, height)
            store_wide(fw, at, rows)
            rows = keep_rows(load_rows(below, at, 2), base + ROWS + half * 2, height)
            store_wide(fw, EDGE + PIX + at, rows)
        aw[4 * COLS:18 * COLS, :] = awi[...]
        slope[4 * COLS:18 * COLS, :] = slopei[...]

        tags = [above[EDGE:BLOCK, :].astype(F32), below[EDGE:BLOCK, :].astype(F32)]
        mine = lab[...].astype(F32)
        lines = [tags[0][0:1, 0:COLS], tags[0][1:2, 0:COLS]]
        lines += [mine[r:r + 1, :] for r in range(ROWS)]
        lines += [tags[1][0:1, 0:COLS], tags[1][1:2, 0:COLS]]
        for r, line in enumerate(lines):
            labs[r // 10, 0:1, (r % 10) * COLS:(r % 10 + 1) * COLS] = line

        def first(t, c):
            at = t * (18 * COLS)
            v = conv_rows(fw, at, 4, k1)
            s = sigmoid(v)
            rows = pl.ds(aligned(at), 4 * COLS)
            slope[rows, :] = (s * (1.0 + v * (1.0 - s))).reshape(4 * COLS, CH)
            store_wide(aw, at, keep_rows(v * s, base - 3 + t * 18, height))
            return c

        lax.fori_loop(0, 2, first, 0)

        small[...] = jnp.zeros_like(small)
        lane = lax.broadcasted_iota(jnp.int32, (1, CH), 1)
        pixel = lax.broadcasted_iota(jnp.int32, (1, 10 * COLS), 1)

        def second(t, c):
            at = t * (10 * COLS)
            v = conv_rows(aw, at, 10, k2)
            s = sigmoid(v)
            act = (v * s).astype(BF16).reshape(10 * COLS, CH)
            logit = lax.dot_general(
                cls[...], act, (((1,), (1,)), ((), ())), preferred_element_type=F32
            )
            rows = [logit[k:k + 1, :] + bias[k:k + 1, 0:1] for k in range(3)]
            top = jnp.maximum(jnp.maximum(rows[0], rows[1]), rows[2])
            ex = [jnp.exp(row - top) for row in rows]
            den = ex[0] + ex[1] + ex[2]
            label = labs[t][0:1, 0:10 * COLS]
            place = pixel + at
            own = jnp.where(jnp.logical_and(place >= 2 * COLS, place < 18 * COLS), 1.0, 0.0)
            dl = [(ex[k] / den - jnp.where(label == k, 1.0, 0.0)) * scale for k in range(3)]
            hi = [d.astype(BF16).astype(F32) for d in dl]
            lo = [d - h for d, h in zip(dl, hi)]
            zero = jnp.zeros((10, 10 * COLS), F32)
            pack = jnp.concatenate(hi + lo + [zero], axis=0)
            back = lax.dot_general(pack.astype(BF16), cls[...], ROWWISE, preferred_element_type=F32)
            grad = back.reshape(10, COLS, CH) * (s * (1.0 + v * (1.0 - s)))
            store_wide(sw, at, keep_rows(grad, base - 2 + t * 10, height))
            part = jnp.dot((pack * own).astype(BF16), act, preferred_element_type=F32)
            sums = [jnp.sum(d * own, axis=1, keepdims=True) for d in dl]
            row = jnp.where(lane == 0, sums[0], jnp.where(lane == 1, sums[1], 0.0))
            small[0:3, :] += part[0:3] + part[3:6]
            small[3:4, :] += jnp.where(lane == 2, sums[2], row)
            return c

        lax.fori_loop(0, 2, second, 0)

        def weight(grad_wide, skip, src, src_skip, out):
            gt[...] = grad_wide[skip * COLS:(skip + ROWS) * COLS, CH:2 * CH].T
            for a in range(3):
                win = src[(src_skip + a) * COLS:(src_skip + a + ROWS) * COLS, :]
                res = jnp.dot(gt[...], win, preferred_element_type=F32)
                for b in range(3):
                    out[(3 * a + b) * CH:(3 * a + b + 1) * CH, :] = (
                        res[:, b * CH:(b + 1) * CH].T.astype(BF16)
                    )

        weight(sw, 2, aw, 2, g2)

        for t in range(6):
            at = t * (3 * COLS)
            v = conv_rows(sw, at, 3, k2t)
            sl = slope[pl.ds(at + 2 * COLS, 3 * COLS), :]
            g = keep_rows(v * sl.reshape(3, COLS, CH), base - 1 + t * 3, height)
            store_wide(fgw, at, g)
        weight(fgw, 1, fw, 3, g1)
        fg[...] = fgw[:, CH:2 * CH]

    return main


def feature_kernel(fg, k1t, out, fgw):
    def widen(t, c):
        store_wide(fgw, t * (2 * COLS), load_rows(fg, t * (2 * COLS), 2))
        return c

    lax.fori_loop(0, 9, widen, 0)

    def step(t, c):
        at = t * (8 * COLS)
        v = conv_rows(fgw, at, 8, k1t)
        out[pl.ds(aligned(at), 8 * COLS), :] = v.astype(BF16).reshape(8 * COLS, CH)
        return c

    lax.fori_loop(0, 2, step, 0)


def convert_out(block, wide, out, sems):
    copies = []
    for t in range(9):
        at = pl.ds(t * CH, CH)
        wide[at, :] = block[at, :].astype(F32)
        copies.append(pltpu.make_async_copy(wide.at[at], out.at[at], sems.at[t]))
        copies[-1].start()
    for copy in copies:
        copy.wait()


def mine_kernel(ids, mine, g1, g2, wide, sems):
    @pl.when(ids[1] == 0)
    def _():
        convert_out(mine, wide, g1, sems)

    @pl.when(ids[1] == 1)
    def _():
        convert_out(mine, wide, g2, sems)


def other_kernel(ids, other, g1_in, g2_in, g1, g2, wide, sems):
    mine_kernel(ids, other, g2, g1, wide, sems)


def ring(step):
    def place(z):
        return (z % 4) * 2 + z // 4

    return [(place(z), place((z + step) % 8)) for z in range(8)]


def shift(value, axis, step, size):
    return lax.ppermute(value, axis, [(i, (i + step) % size) for i in range(size)])


def split_small(small):
    hi = small.astype(BF16)
    return jnp.concatenate([hi, (small - hi.astype(F32)).astype(BF16)], axis=0)


def join_small(rows):
    full = rows.astype(F32)
    return full[..., 0:4, :] + full[..., 4:8, :]


def per_device(features, first_kernel, second_kernel, classifier, class_bias, labels):
    height = ROWS * lax.axis_size(BAND)
    count = height * COLS * lax.axis_size(RAIL)
    scale = float(count) ** (-0.5)
    band = lax.axis_index(BAND)
    core = lax.axis_index("c")
    ids = jnp.stack([band, core])

    flat = features.reshape(PIX, CH)
    lab = labels.reshape(ROWS, COLS)
    k1 = first_kernel.reshape(9 * CH, CH)
    k2 = second_kernel.reshape(9 * CH, CH)
    up, down, fv, labels = call(
        edge_kernel,
        [((BLOCK, CH), BF16), ((BLOCK, CH), BF16), ((PIX, CH), BF16), ((ROWS, COLS), jnp.int32)],
        (flat, lab), [VMEM] * 2, [pltpu.VMEM((16, CH), F32)], limit=8, name="edge",
    )
    above = lax.ppermute(down, DEPTH, ring(1))
    below = lax.ppermute(up, DEPTH, ring(7))

    fwi, awi, slopei, k1t, k2t = call(
        inner_kernel,
        [((PIX, 3 * CH), BF16), ((14 * COLS, 3 * CH), BF16), ((14 * COLS, CH), F32),
         ((9 * CH, CH), BF16), ((9 * CH, CH), BF16)],
        (fv, k1, k2), [VMEM] * 3,
        flops=5_000_000_000, name="inner",
    )

    cls = jnp.pad(jnp.concatenate([classifier.T, classifier.T], axis=0), ((0, 10), (0, 0)))
    bias = jnp.broadcast_to(jnp.pad(class_bias, (0, 5))[:, None], (8, 128))
    g1, g2, small, fg = call(
        make_main(height, scale),
        [((9 * CH, CH), BF16), ((9 * CH, CH), BF16), ((8, CH), F32), ((18 * COLS, CH), BF16)],
        (ids, above, below, fwi, awi, slopei, k1, k2, k2t, cls, bias, labels), [SMEM] + [VMEM] * 11,
        [
            pltpu.VMEM((24 * COLS, 3 * CH), BF16),
            pltpu.VMEM((22 * COLS, 3 * CH), BF16),
            pltpu.VMEM((20 * COLS, 3 * CH), BF16),
            pltpu.VMEM((18 * COLS, 3 * CH), BF16),
            pltpu.VMEM((CH, PIX), BF16),
            pltpu.VMEM((22 * COLS, CH), F32),
            pltpu.VMEM((2, 8, 1024), F32),
        ],
        limit=40, flops=9_000_000_000, name="main",
    )
    (grad_features,) = call(
        feature_kernel, [((PIX, CH), BF16)], (fg, k1t), [VMEM] * 2,
        [pltpu.VMEM((18 * COLS, 3 * CH), BF16)], limit=16, flops=2_500_000_000, name="feature",
    )

    small = small[0:4]
    keep = jnp.where(core == 0, g1, g2)
    give = jnp.where(core == 0, g2, g1)
    tail = jnp.pad(split_small(small), ((0, 8), (0, 0)))
    got = shift(jnp.concatenate([give, tail], axis=0), "c", 1, 2)
    total = (keep.astype(F32) + got[:9 * CH].astype(F32)).astype(BF16)
    small = small + join_small(got[9 * CH:])

    part = 9 * CH // 32
    spread = jnp.concatenate(
        [total.reshape(32, part, CH), jnp.broadcast_to(split_small(small), (32, 8, CH))], axis=1
    )
    spread = lax.all_to_all(spread, PLANE, 0, 0, tiled=True)
    piece = jnp.sum(spread[:, :part].astype(F32), axis=0).astype(BF16)
    small = jnp.sum(join_small(spread[:, part:]), axis=0)

    send = jnp.concatenate([piece, split_small(small)], axis=0)
    one, two, three = [lax.ppermute(send, DEPTH, ring(k)) for k in (2, 4, 6)]

    def four(mine, pick):
        return (mine + pick(two)) + (pick(one) + pick(three))

    small = four(small, lambda block: join_small(block[part:]))
    piece = four(piece.astype(F32), lambda block: block[:part].astype(F32)).astype(BF16)

    full = lax.all_to_all(jnp.broadcast_to(piece, (32, part, CH)), PLANE, 0, 0, tiled=True)
    mine = full.reshape(9 * CH, CH)
    other = shift(mine, "c", 1, 2)
    outs = [((9 * CH, CH), F32)] * 2
    scratch = [pltpu.VMEM((9 * CH, CH), F32), pltpu.SemaphoreType.DMA((9,))]
    halves = call(
        mine_kernel, outs, (ids, mine), [SMEM, VMEM], scratch,
        limit=8, flops=1_000_000_000, name="mine", out_specs=(HBM, HBM),
    )
    grad_first, grad_second = call(
        other_kernel, outs, (ids, other, *halves), [SMEM, VMEM, HBM, HBM], scratch,
        limit=8, name="other", out_specs=(HBM, HBM), aliases={2: 0, 3: 1},
    )
    shape = (3, 3, CH, CH)
    return (
        grad_features.reshape(features.shape), grad_first.reshape(shape), grad_second.reshape(shape),
        small[0:3].T, small[3, 0:3],
    )


def solution(mesh):
    fine = Mesh(mesh.devices.reshape(2, 2, 4, 2, 4, 2), AXES)
    pixels = P(RAIL, BAND, None, None)
    placed = (pixels, P(), P(), P(), P(), P(RAIL, BAND, None))
    return jax.shard_map(
        per_device,
        mesh=fine,
        in_specs=placed,
        out_specs=(pixels, P(), P(), P(), P()),
        check_vma=False,
    )
```

```python
import jax
import jax.numpy as jnp
from jax import lax
from jax.experimental import pallas as pl
from jax.experimental.pallas import tpu as pltpu
from jax.sharding import Mesh, PartitionSpec as P

ROWS = 16
COLS = 96
CH = 256
HALO = 4
PIX = ROWS * COLS
EDGE = HALO * COLS
BLOCK = EDGE + 16
R2 = 10
F32 = jnp.float32
BF16 = jnp.bfloat16
ROWWISE = (((0,), (0,)), ((), ()))
VMEM = pl.BlockSpec(memory_space=pltpu.VMEM)
SMEM = pl.BlockSpec(memory_space=pltpu.SMEM)
HBM = pl.BlockSpec(memory_space=pltpu.HBM)
AXES = ("q", "p", "x", "h", "y", "c")
BAND = ("q", "p")
DEPTH = ("q", "p", "h")
PLANE = ("p", "x", "y")
RAIL = ("x", "h", "y", "c")


def call(kernel, outs, args, ins, scratch=(), limit=24, flops=0, name=None, out_specs=None, aliases={}):
    moved = sum(a.size * a.dtype.itemsize for a in args)
    shapes = tuple(jax.ShapeDtypeStruct(s, d) for s, d in outs)
    return pl.pallas_call(
        kernel,
        out_shape=shapes,
        in_specs=list(ins),
        input_output_aliases=aliases,
        out_specs=(VMEM,) * len(outs) if out_specs is None else out_specs,
        scratch_shapes=list(scratch),
        compiler_params=pltpu.CompilerParams(vmem_limit_bytes=limit * 1024 * 1024),
        cost_estimate=pl.CostEstimate(flops=flops, bytes_accessed=moved, transcendentals=0),
        name=name,
    )(*args)


def aligned(start):
    return start if isinstance(start, int) else pl.multiple_of(start, COLS)


def conv_rows(wide, start, count, kernel):
    patch = jnp.concatenate(
        [wide[pl.ds(aligned(start + a * COLS), count * COLS), :] for a in range(3)], axis=1
    )
    out = jnp.dot(patch, kernel[...], preferred_element_type=F32)
    return out.reshape(count, COLS, CH)


def store_wide(wide, start, rows):
    count = rows.shape[0]
    col = lax.broadcasted_iota(jnp.int32, rows.shape, 1)
    left = jnp.where(col == 0, 0.0, pltpu.roll(rows, 1, 1))
    right = jnp.where(col == COLS - 1, 0.0, pltpu.roll(rows, COLS - 1, 1))
    at = pl.ds(aligned(start), count * COLS)
    wide[at, 0:CH] = left.astype(BF16).reshape(count * COLS, CH)
    wide[at, CH:2 * CH] = rows.astype(BF16).reshape(count * COLS, CH)
    wide[at, 2 * CH:3 * CH] = right.astype(BF16).reshape(count * COLS, CH)


def load_rows(ref, start, count):
    at = pl.ds(aligned(start), count * COLS)
    return ref[at, :].astype(F32).reshape(count, COLS, CH)


def sigmoid(value):
    return 0.5 * jnp.tanh(0.5 * value) + 0.5


def keep_rows(rows, first, height):
    parts = []
    for r in range(rows.shape[0]):
        inside = jnp.logical_and(first + r >= 0, first + r < height)
        parts.append(rows[r] * jnp.where(inside, 1.0, 0.0))
    return jnp.stack(parts)


def edge_kernel(f, lab, up, down, fv, labels, tag):
    for out, row, label in ((up, 0, 0), (down, ROWS - HALO, ROWS - 2)):
        out[0:EDGE, :] = f[row * COLS:(row + HALO) * COLS, :]
        tag[...] = jnp.zeros_like(tag)
        tag[0:2, 0:COLS] = lab[label:label + 2, :].astype(F32)
        out[EDGE:BLOCK, :] = tag[...].astype(BF16)
    fv[...] = f[...]
    labels[...] = lab[...]


def flip(src, dst):
    for t in range(9):
        dst[t * CH:(t + 1) * CH, :] = src[(8 - t) * CH:(9 - t) * CH, :].T


def inner_kernel(f, k1, k2, fw, aw, slope, k2t):
    def widen(t, c):
        store_wide(fw, t * (2 * COLS), load_rows(f, t * (2 * COLS), 2))
        return c

    lax.fori_loop(0, 8, widen, 0)

    for t in range(7):
        at = t * (2 * COLS)
        v = conv_rows(fw, at, 2, k1)
        s = sigmoid(v)
        slope[pl.ds(at, 2 * COLS), :] = (s * (1.0 + v * (1.0 - s))).reshape(2 * COLS, CH)
        store_wide(aw, at, v * s)

    flip(k2, k2t)


def make_main(height, scale):
    def main(ids, bias, above, below, fwi, awi, slopei, k1, k2, k2t, classes, lab, g1, g2, small, fg,
             fw, aw, sw, fgw, gt, slope, labs, held, cls32, cls):
        base = ids[0] * ROWS
        cls32[...] = jnp.zeros_like(cls32)
        cls32[0:3, :] = classes[...].astype(F32)
        cls32[3:6, :] = classes[...].astype(F32)
        cls[...] = cls32[...].astype(BF16)
        fw[EDGE:EDGE + PIX, :] = fwi[...]
        for half in range(2):
            at = half * 2 * COLS
            rows = keep_rows(load_rows(above, at, 2), base - HALO + half * 2, height)
            store_wide(fw, at, rows)
            rows = keep_rows(load_rows(below, at, 2), base + ROWS + half * 2, height)
            store_wide(fw, EDGE + PIX + at, rows)
        aw[4 * COLS:18 * COLS, :] = awi[...]
        slope[4 * COLS:18 * COLS, :] = slopei[...]

        tags = [above[EDGE:BLOCK, :].astype(F32), below[EDGE:BLOCK, :].astype(F32)]
        mine = lab[...].astype(F32)
        lines = [tags[0][0:1, 0:COLS], tags[0][1:2, 0:COLS]]
        lines += [mine[r:r + 1, :] for r in range(ROWS)]
        lines += [tags[1][0:1, 0:COLS], tags[1][1:2, 0:COLS]]
        for r, line in enumerate(lines):
            labs[r // R2, 0:1, (r % R2) * COLS:(r % R2 + 1) * COLS] = line

        def first(t, c):
            at = t * (18 * COLS)
            v = conv_rows(fw, at, 4, k1)
            s = sigmoid(v)
            rows = pl.ds(aligned(at), 4 * COLS)
            slope[rows, :] = (s * (1.0 + v * (1.0 - s))).reshape(4 * COLS, CH)
            store_wide(aw, at, keep_rows(v * s, base - 3 + t * 18, height))
            return c

        lax.fori_loop(0, 2, first, 0)

        small[...] = jnp.zeros_like(small)
        lane = lax.broadcasted_iota(jnp.int32, (1, CH), 1)
        pixel = lax.broadcasted_iota(jnp.int32, (1, R2 * COLS), 1)

        def wide_act(t):
            held[t % 2, :, :] = conv_rows(aw, t * (R2 * COLS), R2, k2).reshape(R2 * COLS, CH)

        def second(t):
            at = t * (R2 * COLS)
            v = held[t % 2, :, :].reshape(R2, COLS, CH)
            s = sigmoid(v)
            act = (v * s).astype(BF16).reshape(R2 * COLS, CH)
            logit = lax.dot_general(
                cls[...], act, (((1,), (1,)), ((), ())), preferred_element_type=F32
            )
            rows = [logit[k:k + 1, :] + bias[k] for k in range(3)]
            top = jnp.maximum(jnp.maximum(rows[0], rows[1]), rows[2])
            ex = [jnp.exp(row - top) for row in rows]
            den = ex[0] + ex[1] + ex[2]
            label = labs[t, 0:1, 0:R2 * COLS]
            place = pixel + at
            own = jnp.where(jnp.logical_and(place >= 2 * COLS, place < 18 * COLS), 1.0, 0.0)
            dl = [(ex[k] / den - jnp.where(label == k, 1.0, 0.0)) * scale for k in range(3)]
            hi = [d.astype(BF16).astype(F32) for d in dl]
            lo = [d - h for d, h in zip(dl, hi)]
            zero = jnp.zeros((10, R2 * COLS), F32)
            pack = jnp.concatenate(hi + lo + [zero], axis=0)
            back = lax.dot_general(pack.astype(BF16), cls[...], ROWWISE, preferred_element_type=F32)
            grad = back.reshape(R2, COLS, CH) * (s * (1.0 + v * (1.0 - s)))
            store_wide(sw, at, keep_rows(grad, base - 2 + t * R2, height))
            part = jnp.dot((pack * own).astype(BF16), act, preferred_element_type=F32)
            sums = [jnp.sum(d * own, axis=1, keepdims=True) for d in dl]
            row = jnp.where(lane == 0, sums[0], jnp.where(lane == 1, sums[1], 0.0))
            small[0:3, :] += part[0:3] + part[3:6]
            small[3:4, :] += jnp.where(lane == 2, sums[2], row)

        N2 = 20 // R2
        for t in range(N2 + 1):
            if t < N2:
                wide_act(t)
            if t > 0:
                second(t - 1)

        def weight(grad_wide, skip, src, src_skip, out):
            gt[...] = grad_wide[skip * COLS:(skip + ROWS) * COLS, CH:2 * CH].T
            for a in range(3):
                win = src[(src_skip + a) * COLS:(src_skip + a + ROWS) * COLS, :]
                res = jnp.dot(gt[...], win, preferred_element_type=F32)
                for b in range(3):
                    out[(3 * a + b) * CH:(3 * a + b + 1) * CH, :] = (
                        res[:, b * CH:(b + 1) * CH].T.astype(BF16)
                    )

        weight(sw, 2, aw, 2, g2)

        for t in range(6):
            at = t * (3 * COLS)
            v = conv_rows(sw, at, 3, k2t)
            sl = slope[pl.ds(at + 2 * COLS, 3 * COLS), :]
            g = keep_rows(v * sl.reshape(3, COLS, CH), base - 1 + t * 3, height)
            store_wide(fgw, at, g)
        weight(fgw, 1, fw, 3, g1)
        fg[...] = fgw[:, CH:2 * CH]

    return main


def feature_kernel(fg, k1, sums, out, classes, bias, fgw, k1t):
    classes[...] = sums[0:3, :]
    bias[...] = sums[3:4, 0:3]
    flip(k1, k1t)

    def widen(t, c):
        store_wide(fgw, t * (2 * COLS), load_rows(fg, t * (2 * COLS), 2))
        return c

    lax.fori_loop(0, 9, widen, 0)

    def step(t, c):
        at = t * (8 * COLS)
        v = conv_rows(fgw, at, 8, k1t)
        out[pl.ds(aligned(at), 8 * COLS), :] = v.astype(BF16).reshape(8 * COLS, CH)
        return c

    lax.fori_loop(0, 2, step, 0)


def convert_out(block, wide, out, row, sems):
    copies = []
    for t in range(block.shape[0] // 384):
        at = pl.ds(t * 384, 384)
        wide[at, :] = block[at, :].astype(F32)
        copies.append(pltpu.make_async_copy(wide.at[at], out.at[pl.ds(row + t * 384, 384)], sems.at[t]))
        copies[-1].start()
    for copy in copies:
        copy.wait()


def mine_kernel(ids, mine, g1, g2, wide, sems, row=0):
    @pl.when(ids[1] == 0)
    def _():
        convert_out(mine, wide, g1, row, sems)

    @pl.when(ids[1] == 1)
    def _():
        convert_out(mine, wide, g2, row, sems)


def other_kernel(row):
    def other(ids, block, g1_in, g2_in, g1, g2, wide, sems):
        mine_kernel(ids, block, g2, g1, wide, sems, row)

    return other


def ring(step):
    def place(z):
        return (z % 4) * 2 + z // 4

    return [(place(z), place((z + step) % 8)) for z in range(8)]


def shift(value, axis, step, size):
    return lax.ppermute(value, axis, [(i, (i + step) % size) for i in range(size)])


def split_small(small):
    hi = small.astype(BF16)
    return jnp.concatenate([hi, (small - hi.astype(F32)).astype(BF16)], axis=0)


def join_small(rows):
    full = rows.astype(F32)
    return full[..., 0:4, :] + full[..., 4:8, :]


def per_device(features, first_kernel, second_kernel, classifier, class_bias, labels):
    height = ROWS * lax.axis_size(BAND)
    count = height * COLS * lax.axis_size(RAIL)
    scale = float(count) ** (-0.5)
    band = lax.axis_index(BAND)
    core = lax.axis_index("c")
    ids = jnp.stack([band, core])

    flat = features.reshape(PIX, CH)
    lab = labels.reshape(ROWS, COLS)
    k1 = first_kernel.reshape(9 * CH, CH)
    k2 = second_kernel.reshape(9 * CH, CH)
    up, down, fv, labels = call(
        edge_kernel,
        [((BLOCK, CH), BF16), ((BLOCK, CH), BF16), ((PIX, CH), BF16), ((ROWS, COLS), jnp.int32)],
        (flat, lab), [VMEM] * 2, [pltpu.VMEM((16, CH), F32)], limit=8, name="edge",
    )
    above = lax.ppermute(down, DEPTH, ring(1))
    below = lax.ppermute(up, DEPTH, ring(7))

    fwi, awi, slopei, k2t = call(
        inner_kernel,
        [((PIX, 3 * CH), BF16), ((14 * COLS, 3 * CH), BF16), ((14 * COLS, CH), F32),
         ((9 * CH, CH), BF16)],
        (fv, k1, k2), [VMEM] * 3,
        flops=5_000_000_000, name="inner",
    )

    g1, g2, small, fg = call(
        make_main(height, scale),
        [((9 * CH, CH), BF16), ((9 * CH, CH), BF16), ((8, CH), F32), ((18 * COLS, CH), BF16)],
        (ids, class_bias, above, below, fwi, awi, slopei, k1, k2, k2t, classifier.T, labels),
        [SMEM] * 2 + [VMEM] * 10,
        [
            pltpu.VMEM((24 * COLS, 3 * CH), BF16),
            pltpu.VMEM((22 * COLS, 3 * CH), BF16),
            pltpu.VMEM((20 * COLS, 3 * CH), BF16),
            pltpu.VMEM((18 * COLS, 3 * CH), BF16),
            pltpu.VMEM((CH, PIX), BF16),
            pltpu.VMEM((22 * COLS, CH), F32),
            pltpu.VMEM((20 // R2, 8, 1024), F32),
            pltpu.VMEM((2, R2 * COLS, CH), F32),
            pltpu.VMEM((16, CH), F32),
            pltpu.VMEM((16, CH), BF16),
        ],
        limit=40, flops=9_000_000_000, name="main",
    )
    small = small[0:4]
    keep = jnp.where(core == 0, g1, g2)
    give = jnp.where(core == 0, g2, g1)
    tail = jnp.pad(split_small(small), ((0, 8), (0, 0)))
    got = shift(jnp.concatenate([give, tail], axis=0), "c", 1, 2)
    total = (keep.astype(F32) + got[:9 * CH].astype(F32)).astype(BF16)
    small = small + join_small(got[9 * CH:])

    part = 9 * CH // 32
    spread = jnp.concatenate(
        [total.reshape(32, part, CH), jnp.broadcast_to(split_small(small), (32, 8, CH))], axis=1
    )
    spread = lax.all_to_all(spread, PLANE, 0, 0, tiled=True)
    piece = jnp.sum(spread[:, :part].astype(F32), axis=0).astype(BF16)
    small = jnp.sum(join_small(spread[:, part:]), axis=0)

    send = jnp.concatenate([piece, split_small(small)], axis=0)
    one, two, three = [lax.ppermute(send, DEPTH, ring(k)) for k in (2, 4, 6)]

    def four(mine, pick):
        return (mine + pick(two)) + (pick(one) + pick(three))

    small = four(small, lambda block: join_small(block[part:]))
    piece = four(piece.astype(F32), lambda block: block[:part].astype(F32)).astype(BF16)

    grad_features, grad_classifier, grad_bias = call(
        feature_kernel, [((PIX, CH), BF16), ((3, CH), F32), ((1, 3), F32)], (fg, k1, small), [VMEM] * 3,
        [pltpu.VMEM((18 * COLS, 3 * CH), BF16), pltpu.VMEM((9 * CH, CH), BF16)],
        limit=16, flops=2_500_000_000, name="feature",
    )
    full = lax.all_to_all(jnp.broadcast_to(piece, (32, part, CH)), PLANE, 0, 0, tiled=True)
    full, grad_features = lax.optimization_barrier((full, grad_features))
    mine = full.reshape(9 * CH, CH)
    half = 9 * CH // 2
    others = [shift(mine[k * half:(k + 1) * half], "c", 1, 2) for k in range(2)]
    outs = [((9 * CH, CH), F32)] * 2
    scratch = [pltpu.VMEM((9 * CH, CH), F32), pltpu.SemaphoreType.DMA((6,))]
    grads = call(
        mine_kernel, outs, (ids, mine), [SMEM, VMEM], scratch,
        limit=8, flops=1_000_000_000, name="mine", out_specs=(HBM, HBM),
    )
    for k, other in enumerate(others):
        grads = call(
            other_kernel(k * half), outs, (ids, other, *grads), [SMEM, VMEM, HBM, HBM], scratch,
            limit=8, name="other", out_specs=(HBM, HBM), aliases={2: 0, 3: 1},
        )
    grad_first, grad_second = grads
    shape = (3, 3, CH, CH)
    return (
        grad_features.reshape(features.shape), grad_first.reshape(shape), grad_second.reshape(shape),
        grad_classifier.T, grad_bias[0],
    )


def solution(mesh):
    fine = Mesh(mesh.devices.reshape(2, 2, 4, 2, 4, 2), AXES)
    pixels = P(RAIL, BAND, None, None)
    placed = (pixels, P(), P(), P(), P(), P(RAIL, BAND, None))
    return jax.shard_map(
        per_device,
        mesh=fine,
        in_specs=placed,
        out_specs=(pixels, P(), P(), P(), P()),
        check_vma=False,
    )
```

```python
import jax
import jax.numpy as jnp
from jax import lax
from jax.experimental import pallas as pl
from jax.experimental.pallas import tpu as pltpu
from jax.sharding import Mesh, PartitionSpec as P

ROWS = 16
COLS = 96
CH = 256
HALO = 4
PIX = ROWS * COLS
EDGE = HALO * COLS
BLOCK = EDGE + 16
R2 = 10
F32 = jnp.float32
BF16 = jnp.bfloat16
ROWWISE = (((0,), (0,)), ((), ()))
VMEM = pl.BlockSpec(memory_space=pltpu.VMEM)
SMEM = pl.BlockSpec(memory_space=pltpu.SMEM)
HBM = pl.BlockSpec(memory_space=pltpu.HBM)
AXES = ("q", "p", "x", "h", "y", "c")
BAND = ("q", "p")
DEPTH = ("q", "p", "h")
PLANE = ("p", "x", "y")
RAIL = ("x", "h", "y", "c")


def call(kernel, outs, args, ins, scratch=(), limit=24, flops=0, name=None, out_specs=None, aliases={}):
    moved = sum(a.size * a.dtype.itemsize for a in args)
    shapes = tuple(jax.ShapeDtypeStruct(s, d) for s, d in outs)
    return pl.pallas_call(
        kernel,
        out_shape=shapes,
        in_specs=list(ins),
        input_output_aliases=aliases,
        out_specs=(VMEM,) * len(outs) if out_specs is None else out_specs,
        scratch_shapes=list(scratch),
        compiler_params=pltpu.CompilerParams(vmem_limit_bytes=limit * 1024 * 1024),
        cost_estimate=pl.CostEstimate(flops=flops, bytes_accessed=moved, transcendentals=0),
        name=name,
    )(*args)


def aligned(start):
    return start if isinstance(start, int) else pl.multiple_of(start, COLS)


def conv_rows(wide, start, count, kernel):
    patch = jnp.concatenate(
        [wide[pl.ds(aligned(start + a * COLS), count * COLS), :] for a in range(3)], axis=1
    )
    out = jnp.dot(patch, kernel[...], preferred_element_type=F32)
    return out.reshape(count, COLS, CH)


def store_wide(wide, start, rows):
    count = rows.shape[0]
    col = lax.broadcasted_iota(jnp.int32, rows.shape, 1)
    left = jnp.where(col == 0, 0.0, pltpu.roll(rows, 1, 1))
    right = jnp.where(col == COLS - 1, 0.0, pltpu.roll(rows, COLS - 1, 1))
    at = pl.ds(aligned(start), count * COLS)
    wide[at, 0:CH] = left.astype(BF16).reshape(count * COLS, CH)
    wide[at, CH:2 * CH] = rows.astype(BF16).reshape(count * COLS, CH)
    wide[at, 2 * CH:3 * CH] = right.astype(BF16).reshape(count * COLS, CH)


def load_rows(ref, start, count):
    at = pl.ds(aligned(start), count * COLS)
    return ref[at, :].astype(F32).reshape(count, COLS, CH)


def sigmoid(value):
    return 0.5 * jnp.tanh(0.5 * value) + 0.5


def keep_rows(rows, first, height):
    parts = []
    for r in range(rows.shape[0]):
        inside = jnp.logical_and(first + r >= 0, first + r < height)
        parts.append(rows[r] * jnp.where(inside, 1.0, 0.0))
    return jnp.stack(parts)


def edge_kernel(f, lab, up, down, fv, labels, tag):
    for out, row, label in ((up, 0, 0), (down, ROWS - HALO, ROWS - 2)):
        out[0:EDGE, :] = f[row * COLS:(row + HALO) * COLS, :]
        tag[...] = jnp.zeros_like(tag)
        tag[0:2, 0:COLS] = lab[label:label + 2, :].astype(F32)
        out[EDGE:BLOCK, :] = tag[...].astype(BF16)
    fv[...] = f[...]
    labels[...] = lab[...]


def flip(src, dst):
    for t in range(9):
        dst[t * CH:(t + 1) * CH, :] = src[(8 - t) * CH:(9 - t) * CH, :].T


def inner_kernel(f, k1, k2, fw, aw, slope, k2t):
    def widen(t, c):
        store_wide(fw, t * (2 * COLS), load_rows(f, t * (2 * COLS), 2))
        return c

    lax.fori_loop(0, 8, widen, 0)

    for t in range(7):
        at = t * (2 * COLS)
        v = conv_rows(fw, at, 2, k1)
        s = sigmoid(v)
        slope[pl.ds(at, 2 * COLS), :] = (s * (1.0 + v * (1.0 - s))).reshape(2 * COLS, CH)
        store_wide(aw, at, v * s)

    flip(k2, k2t)


def make_main(height, scale):
    def main(ids, bias, above, below, fwi, awi, slopei, k1, k2, k2t, classes, lab, g1, g2, small, fg,
             fw, aw, sw, fgw, gt, slope, labs, held, cls32, cls):
        base = ids[0] * ROWS
        cls32[...] = jnp.zeros_like(cls32)
        cls32[0:3, :] = classes[...].astype(F32)
        cls32[3:6, :] = classes[...].astype(F32)
        cls[...] = cls32[...].astype(BF16)
        fw[EDGE:EDGE + PIX, :] = fwi[...]
        for half in range(2):
            at = half * 2 * COLS
            rows = keep_rows(load_rows(above, at, 2), base - HALO + half * 2, height)
            store_wide(fw, at, rows)
            rows = keep_rows(load_rows(below, at, 2), base + ROWS + half * 2, height)
            store_wide(fw, EDGE + PIX + at, rows)
        aw[4 * COLS:18 * COLS, :] = awi[...]
        slope[4 * COLS:18 * COLS, :] = slopei[...]

        tags = [above[EDGE:BLOCK, :].astype(F32), below[EDGE:BLOCK, :].astype(F32)]
        mine = lab[...].astype(F32)
        lines = [tags[0][0:1, 0:COLS], tags[0][1:2, 0:COLS]]
        lines += [mine[r:r + 1, :] for r in range(ROWS)]
        lines += [tags[1][0:1, 0:COLS], tags[1][1:2, 0:COLS]]
        for r, line in enumerate(lines):
            labs[r // R2, 0:1, (r % R2) * COLS:(r % R2 + 1) * COLS] = line

        def first(t, c):
            at = t * (18 * COLS)
            v = conv_rows(fw, at, 4, k1)
            s = sigmoid(v)
            rows = pl.ds(aligned(at), 4 * COLS)
            slope[rows, :] = (s * (1.0 + v * (1.0 - s))).reshape(4 * COLS, CH)
            store_wide(aw, at, keep_rows(v * s, base - 3 + t * 18, height))
            return c

        lax.fori_loop(0, 2, first, 0)

        small[...] = jnp.zeros_like(small)
        lane = lax.broadcasted_iota(jnp.int32, (1, CH), 1)
        pixel = lax.broadcasted_iota(jnp.int32, (1, R2 * COLS), 1)

        def wide_act(t):
            held[t % 2, :, :] = conv_rows(aw, t * (R2 * COLS), R2, k2).reshape(R2 * COLS, CH)

        def second(t):
            at = t * (R2 * COLS)
            v = held[t % 2, :, :].reshape(R2, COLS, CH)
            s = sigmoid(v)
            act = (v * s).astype(BF16).reshape(R2 * COLS, CH)
            logit = lax.dot_general(
                cls[...], act, (((1,), (1,)), ((), ())), preferred_element_type=F32
            )
            rows = [logit[k:k + 1, :] + bias[k] for k in range(3)]
            top = jnp.maximum(jnp.maximum(rows[0], rows[1]), rows[2])
            ex = [jnp.exp(row - top) for row in rows]
            den = ex[0] + ex[1] + ex[2]
            label = labs[t, 0:1, 0:R2 * COLS]
            place = pixel + at
            own = jnp.where(jnp.logical_and(place >= 2 * COLS, place < 18 * COLS), 1.0, 0.0)
            dl = [(ex[k] / den - jnp.where(label == k, 1.0, 0.0)) * scale for k in range(3)]
            hi = [d.astype(BF16).astype(F32) for d in dl]
            lo = [d - h for d, h in zip(dl, hi)]
            zero = jnp.zeros((10, R2 * COLS), F32)
            pack = jnp.concatenate(hi + lo + [zero], axis=0)
            back = lax.dot_general(pack.astype(BF16), cls[...], ROWWISE, preferred_element_type=F32)
            grad = back.reshape(R2, COLS, CH) * (s * (1.0 + v * (1.0 - s)))
            store_wide(sw, at, keep_rows(grad, base - 2 + t * R2, height))
            part = jnp.dot((pack * own).astype(BF16), act, preferred_element_type=F32)
            sums = [jnp.sum(d * own, axis=1, keepdims=True) for d in dl]
            row = jnp.where(lane == 0, sums[0], jnp.where(lane == 1, sums[1], 0.0))
            small[0:3, :] += part[0:3] + part[3:6]
            small[3:4, :] += jnp.where(lane == 2, sums[2], row)

        N2 = 20 // R2
        for t in range(N2 + 1):
            if t < N2:
                wide_act(t)
            if t > 0:
                second(t - 1)

        def weight(grad_wide, skip, src, src_skip, out):
            gt[...] = grad_wide[skip * COLS:(skip + ROWS) * COLS, CH:2 * CH].T
            for a in range(3):
                win = src[(src_skip + a) * COLS:(src_skip + a + ROWS) * COLS, :]
                res = jnp.dot(gt[...], win, preferred_element_type=F32)
                for b in range(3):
                    out[(3 * a + b) * CH:(3 * a + b + 1) * CH, :] = (
                        res[:, b * CH:(b + 1) * CH].T.astype(BF16)
                    )

        weight(sw, 2, aw, 2, g2)

        for t in range(6):
            at = t * (3 * COLS)
            v = conv_rows(sw, at, 3, k2t)
            sl = slope[pl.ds(at + 2 * COLS, 3 * COLS), :]
            g = keep_rows(v * sl.reshape(3, COLS, CH), base - 1 + t * 3, height)
            store_wide(fgw, at, g)
        weight(fgw, 1, fw, 3, g1)
        fg[...] = fgw[:, CH:2 * CH]

    return main


def feature_kernel(fg, k1, sums, out, classes, bias, fgw, k1t):
    classes[...] = sums[0:3, :]
    bias[...] = sums[3:4, 0:3]
    flip(k1, k1t)

    def widen(t, c):
        store_wide(fgw, t * (2 * COLS), load_rows(fg, t * (2 * COLS), 2))
        return c

    lax.fori_loop(0, 9, widen, 0)

    def step(t, c):
        at = t * (8 * COLS)
        v = conv_rows(fgw, at, 8, k1t)
        out[pl.ds(aligned(at), 8 * COLS), :] = v.astype(BF16).reshape(8 * COLS, CH)
        return c

    lax.fori_loop(0, 2, step, 0)


def convert_out(block, wide, out, sems):
    copies = []
    for t in range(6):
        at = pl.ds(t * 384, 384)
        wide[at, :] = block[at, :].astype(F32)
        copies.append(pltpu.make_async_copy(wide.at[at], out.at[at], sems.at[t]))
        copies[-1].start()
    for copy in copies:
        copy.wait()


def mine_kernel(ids, mine, g1, g2, wide, sems):
    @pl.when(ids[1] == 0)
    def _():
        convert_out(mine, wide, g1, sems)

    @pl.when(ids[1] == 1)
    def _():
        convert_out(mine, wide, g2, sems)


def other_kernel(ids, other, g1_in, g2_in, g1, g2, wide, sems):
    mine_kernel(ids, other, g2, g1, wide, sems)


def ring(step):
    def place(z):
        return (z % 4) * 2 + z // 4

    return [(place(z), place((z + step) % 8)) for z in range(8)]


def shift(value, axis, step, size):
    return lax.ppermute(value, axis, [(i, (i + step) % size) for i in range(size)])


def split_small(small):
    hi = small.astype(BF16)
    return jnp.concatenate([hi, (small - hi.astype(F32)).astype(BF16)], axis=0)


def join_small(rows):
    full = rows.astype(F32)
    return full[..., 0:4, :] + full[..., 4:8, :]


def per_device(features, first_kernel, second_kernel, classifier, class_bias, labels):
    height = ROWS * lax.axis_size(BAND)
    count = height * COLS * lax.axis_size(RAIL)
    scale = float(count) ** (-0.5)
    band = lax.axis_index(BAND)
    core = lax.axis_index("c")
    ids = jnp.stack([band, core])

    flat = features.reshape(PIX, CH)
    lab = labels.reshape(ROWS, COLS)
    k1 = first_kernel.reshape(9 * CH, CH)
    k2 = second_kernel.reshape(9 * CH, CH)
    up, down, fv, labels = call(
        edge_kernel,
        [((BLOCK, CH), BF16), ((BLOCK, CH), BF16), ((PIX, CH), BF16), ((ROWS, COLS), jnp.int32)],
        (flat, lab), [VMEM] * 2, [pltpu.VMEM((16, CH), F32)], limit=8, name="edge",
    )
    first = core == 0
    up, down, ids, first = lax.optimization_barrier((up, down, ids, first))
    above = lax.ppermute(down, DEPTH, ring(1))
    below = lax.ppermute(up, DEPTH, ring(7))

    fwi, awi, slopei, k2t = call(
        inner_kernel,
        [((PIX, 3 * CH), BF16), ((14 * COLS, 3 * CH), BF16), ((14 * COLS, CH), F32),
         ((9 * CH, CH), BF16)],
        (fv, k1, k2), [VMEM] * 3,
        flops=5_000_000_000, limit=12, name="inner",
    )

    g1, g2, small, fg = call(
        make_main(height, scale),
        [((9 * CH, CH), BF16), ((9 * CH, CH), BF16), ((8, CH), F32), ((18 * COLS, CH), BF16)],
        (ids, class_bias, above, below, fwi, awi, slopei, k1, k2, k2t, classifier.T, labels),
        [SMEM] * 2 + [VMEM] * 10,
        [
            pltpu.VMEM((24 * COLS, 3 * CH), BF16),
            pltpu.VMEM((22 * COLS, 3 * CH), BF16),
            pltpu.VMEM((20 * COLS, 3 * CH), BF16),
            pltpu.VMEM((18 * COLS, 3 * CH), BF16),
            pltpu.VMEM((CH, PIX), BF16),
            pltpu.VMEM((22 * COLS, CH), F32),
            pltpu.VMEM((20 // R2, 8, 1024), F32),
            pltpu.VMEM((2, R2 * COLS, CH), F32),
            pltpu.VMEM((16, CH), F32),
            pltpu.VMEM((16, CH), BF16),
        ],
        limit=22, flops=9_000_000_000, name="main",
    )
    small = small[0:4]
    keep = jnp.where(first, g1, g2)
    give = jnp.where(first, g2, g1)
    tail = jnp.pad(split_small(small), ((0, 8), (0, 0)))
    got = shift(jnp.concatenate([give, tail], axis=0), "c", 1, 2)
    total = (keep.astype(F32) + got[:9 * CH].astype(F32)).astype(BF16)
    small = small + join_small(got[9 * CH:])

    part = 9 * CH // 32
    spread = jnp.concatenate(
        [total.reshape(32, part, CH), jnp.broadcast_to(split_small(small), (32, 8, CH))], axis=1
    )
    spread = lax.all_to_all(spread, PLANE, 0, 0, tiled=True)
    piece = jnp.sum(spread[:, :part].astype(F32), axis=0).astype(BF16)
    small = jnp.sum(join_small(spread[:, part:]), axis=0)

    send = jnp.concatenate([piece, split_small(small)], axis=0)
    one, two, three = [lax.ppermute(send, DEPTH, ring(k)) for k in (2, 4, 6)]

    def four(mine, pick):
        return (mine + pick(two)) + (pick(one) + pick(three))

    small = four(small, lambda block: join_small(block[part:]))
    piece = four(piece.astype(F32), lambda block: block[:part].astype(F32)).astype(BF16)

    grad_features, grad_classifier, grad_bias = call(
        feature_kernel, [((PIX, CH), BF16), ((3, CH), F32), ((1, 3), F32)], (fg, k1, small), [VMEM] * 3,
        [pltpu.VMEM((18 * COLS, 3 * CH), BF16), pltpu.VMEM((9 * CH, CH), BF16)],
        limit=12, flops=2_500_000_000, name="feature",
    )
    full = lax.all_to_all(jnp.broadcast_to(piece, (32, part, CH)), PLANE, 0, 0, tiled=True)
    full, grad_features = lax.optimization_barrier((full, grad_features))
    mine = full.reshape(9 * CH, CH)
    other = shift(mine, "c", 1, 2)
    outs = [((9 * CH, CH), F32)] * 2
    scratch = [pltpu.VMEM((9 * CH, CH), F32), pltpu.SemaphoreType.DMA((6,))]
    halves = call(
        mine_kernel, outs, (ids, mine), [SMEM, VMEM], scratch,
        limit=8, flops=1_000_000_000, name="mine", out_specs=(HBM, HBM),
    )
    grad_first, grad_second = call(
        other_kernel, outs, (ids, other, *halves), [SMEM, VMEM, HBM, HBM], scratch,
        limit=8, name="other", out_specs=(HBM, HBM), aliases={2: 0, 3: 1},
    )
    shape = (3, 3, CH, CH)
    return (
        grad_features.reshape(features.shape), grad_first.reshape(shape), grad_second.reshape(shape),
        grad_classifier.T, grad_bias[0],
    )


def solution(mesh):
    fine = Mesh(mesh.devices.reshape(2, 2, 4, 2, 4, 2), AXES)
    pixels = P(RAIL, BAND, None, None)
    placed = (pixels, P(), P(), P(), P(), P(RAIL, BAND, None))
    return jax.shard_map(
        per_device,
        mesh=fine,
        in_specs=placed,
        out_specs=(pixels, P(), P(), P(), P()),
        check_vma=False,
    )
```

```python
import jax
import jax.numpy as jnp
from jax import lax
from jax.experimental import pallas as pl
from jax.experimental.pallas import tpu as pltpu
from jax.sharding import Mesh, PartitionSpec as P

ROWS = 16
COLS = 96
CH = 256
HALO = 4
PIX = ROWS * COLS
EDGE = HALO * COLS
BLOCK = EDGE + 16
R2 = 10
F32 = jnp.float32
BF16 = jnp.bfloat16
ROWWISE = (((0,), (0,)), ((), ()))
VMEM = pl.BlockSpec(memory_space=pltpu.VMEM)
HBM = pl.BlockSpec(memory_space=pltpu.HBM)
AXES = ("q", "p", "x", "h", "y", "c")
BAND = ("q", "p")
DEPTH = ("q", "p", "h")
PLANE = ("p", "x", "y")
RAIL = ("x", "h", "y", "c")


def call(kernel, outs, args, ins, scratch=(), limit=24, flops=0, name=None, out_specs=None, aliases={}):
    moved = sum(a.size * a.dtype.itemsize for a in args)
    shapes = tuple(jax.ShapeDtypeStruct(s, d) for s, d in outs)
    return pl.pallas_call(
        kernel,
        out_shape=shapes,
        in_specs=list(ins),
        input_output_aliases=aliases,
        out_specs=(VMEM,) * len(outs) if out_specs is None else out_specs,
        scratch_shapes=list(scratch),
        compiler_params=pltpu.CompilerParams(vmem_limit_bytes=limit * 1024 * 1024),
        cost_estimate=pl.CostEstimate(flops=flops, bytes_accessed=moved, transcendentals=0),
        name=name,
    )(*args)


def aligned(start):
    return start if isinstance(start, int) else pl.multiple_of(start, COLS)


def conv_rows(wide, start, count, kernel):
    patch = jnp.concatenate(
        [wide[pl.ds(aligned(start + a * COLS), count * COLS), :] for a in range(3)], axis=1
    )
    out = jnp.dot(patch, kernel[...], preferred_element_type=F32)
    return out.reshape(count, COLS, CH)


def store_wide(wide, start, rows):
    count = rows.shape[0]
    col = lax.broadcasted_iota(jnp.int32, rows.shape, 1)
    left = jnp.where(col == 0, 0.0, pltpu.roll(rows, 1, 1))
    right = jnp.where(col == COLS - 1, 0.0, pltpu.roll(rows, COLS - 1, 1))
    at = pl.ds(aligned(start), count * COLS)
    wide[at, 0:CH] = left.astype(BF16).reshape(count * COLS, CH)
    wide[at, CH:2 * CH] = rows.astype(BF16).reshape(count * COLS, CH)
    wide[at, 2 * CH:3 * CH] = right.astype(BF16).reshape(count * COLS, CH)


def load_rows(ref, start, count):
    at = pl.ds(aligned(start), count * COLS)
    return ref[at, :].astype(F32).reshape(count, COLS, CH)


def sigmoid(value):
    return 0.5 * jnp.tanh(0.5 * value) + 0.5


def keep_rows(rows, first, height):
    parts = []
    for r in range(rows.shape[0]):
        inside = jnp.logical_and(first + r >= 0, first + r < height)
        parts.append(rows[r] * jnp.where(inside, 1.0, 0.0))
    return jnp.stack(parts)


def edge_kernel(f, lab, up, down, fv, labels, tag):
    for out, row, label in ((up, 0, 0), (down, ROWS - HALO, ROWS - 2)):
        out[0:EDGE, :] = f[row * COLS:(row + HALO) * COLS, :]
        tag[...] = jnp.zeros_like(tag)
        tag[0:2, 0:COLS] = lab[label:label + 2, :].astype(F32)
        out[EDGE:BLOCK, :] = tag[...].astype(BF16)
    fv[...] = f[...]
    labels[...] = lab[...]


def flip(src, dst):
    for t in range(9):
        dst[t * CH:(t + 1) * CH, :] = src[(8 - t) * CH:(9 - t) * CH, :].T


def inner_kernel(f, k1, k2, fw, aw, slope, k2t):
    def widen(t, c):
        store_wide(fw, t * (2 * COLS), load_rows(f, t * (2 * COLS), 2))
        return c

    lax.fori_loop(0, 8, widen, 0)

    for t in range(7):
        at = t * (2 * COLS)
        v = conv_rows(fw, at, 2, k1)
        s = sigmoid(v)
        slope[pl.ds(at, 2 * COLS), :] = (s * (1.0 + v * (1.0 - s))).reshape(2 * COLS, CH)
        store_wide(aw, at, v * s)

    flip(k2, k2t)


def make_main(height, scale):
    def main(bias, above, below, fwi, awi, slopei, k1, k2, k2t, classes, lab, g1, g2, small, fg,
             fw, aw, sw, fgw, gt, slope, labs, held, cls32, cls):
        base = (lax.axis_index("q") * 2 + lax.axis_index("p")) * ROWS
        cls32[...] = jnp.zeros_like(cls32)
        cls32[0:3, :] = classes[...].astype(F32)
        cls32[3:6, :] = classes[...].astype(F32)
        cls[...] = cls32[...].astype(BF16)
        fw[EDGE:EDGE + PIX, :] = fwi[...]
        for half in range(2):
            at = half * 2 * COLS
            rows = keep_rows(load_rows(above, at, 2), base - HALO + half * 2, height)
            store_wide(fw, at, rows)
            rows = keep_rows(load_rows(below, at, 2), base + ROWS + half * 2, height)
            store_wide(fw, EDGE + PIX + at, rows)
        aw[4 * COLS:18 * COLS, :] = awi[...]
        slope[4 * COLS:18 * COLS, :] = slopei[...]

        tags = [above[EDGE:BLOCK, :].astype(F32), below[EDGE:BLOCK, :].astype(F32)]
        mine = lab[...].astype(F32)
        lines = [tags[0][0:1, 0:COLS], tags[0][1:2, 0:COLS]]
        lines += [mine[r:r + 1, :] for r in range(ROWS)]
        lines += [tags[1][0:1, 0:COLS], tags[1][1:2, 0:COLS]]
        for r, line in enumerate(lines):
            labs[r // R2, 0:1, (r % R2) * COLS:(r % R2 + 1) * COLS] = line

        def first(t, c):
            at = t * (18 * COLS)
            v = conv_rows(fw, at, 4, k1)
            s = sigmoid(v)
            rows = pl.ds(aligned(at), 4 * COLS)
            slope[rows, :] = (s * (1.0 + v * (1.0 - s))).reshape(4 * COLS, CH)
            store_wide(aw, at, keep_rows(v * s, base - 3 + t * 18, height))
            return c

        lax.fori_loop(0, 2, first, 0)

        small[...] = jnp.zeros_like(small)
        lane = lax.broadcasted_iota(jnp.int32, (1, CH), 1)
        pixel = lax.broadcasted_iota(jnp.int32, (1, R2 * COLS), 1)

        def wide_act(t):
            held[t % 2, :, :] = conv_rows(aw, t * (R2 * COLS), R2, k2).reshape(R2 * COLS, CH)

        def second(t):
            at = t * (R2 * COLS)
            v = held[t % 2, :, :].reshape(R2, COLS, CH)
            s = sigmoid(v)
            act = (v * s).astype(BF16).reshape(R2 * COLS, CH)
            logit = lax.dot_general(
                cls[...], act, (((1,), (1,)), ((), ())), preferred_element_type=F32
            )
            rows = [logit[k:k + 1, :] + bias[0:1, k:k + 1] for k in range(3)]
            top = jnp.maximum(jnp.maximum(rows[0], rows[1]), rows[2])
            ex = [jnp.exp(row - top) for row in rows]
            den = ex[0] + ex[1] + ex[2]
            label = labs[t, 0:1, 0:R2 * COLS]
            place = pixel + at
            own = jnp.where(jnp.logical_and(place >= 2 * COLS, place < 18 * COLS), 1.0, 0.0)
            dl = [(ex[k] / den - jnp.where(label == k, 1.0, 0.0)) * scale for k in range(3)]
            hi = [d.astype(BF16).astype(F32) for d in dl]
            lo = [d - h for d, h in zip(dl, hi)]
            zero = jnp.zeros((10, R2 * COLS), F32)
            pack = jnp.concatenate(hi + lo + [zero], axis=0)
            back = lax.dot_general(pack.astype(BF16), cls[...], ROWWISE, preferred_element_type=F32)
            grad = back.reshape(R2, COLS, CH) * (s * (1.0 + v * (1.0 - s)))
            store_wide(sw, at, keep_rows(grad, base - 2 + t * R2, height))
            part = jnp.dot((pack * own).astype(BF16), act, preferred_element_type=F32)
            sums = [jnp.sum(d * own, axis=1, keepdims=True) for d in dl]
            row = jnp.where(lane == 0, sums[0], jnp.where(lane == 1, sums[1], 0.0))
            small[0:3, :] += part[0:3] + part[3:6]
            small[3:4, :] += jnp.where(lane == 2, sums[2], row)

        N2 = 20 // R2
        for t in range(N2 + 1):
            if t < N2:
                wide_act(t)
            if t > 0:
                second(t - 1)

        def weight(grad_wide, skip, src, src_skip, out):
            gt[...] = grad_wide[skip * COLS:(skip + ROWS) * COLS, CH:2 * CH].T
            for a in range(3):
                win = src[(src_skip + a) * COLS:(src_skip + a + ROWS) * COLS, :]
                res = jnp.dot(gt[...], win, preferred_element_type=F32)
                for b in range(3):
                    out[(3 * a + b) * CH:(3 * a + b + 1) * CH, :] = (
                        res[:, b * CH:(b + 1) * CH].T.astype(BF16)
                    )

        weight(sw, 2, aw, 2, g2)

        for t in range(6):
            at = t * (3 * COLS)
            v = conv_rows(sw, at, 3, k2t)
            sl = slope[pl.ds(at + 2 * COLS, 3 * COLS), :]
            g = keep_rows(v * sl.reshape(3, COLS, CH), base - 1 + t * 3, height)
            store_wide(fgw, at, g)
        weight(fgw, 1, fw, 3, g1)
        fg[...] = fgw[:, CH:2 * CH]

    return main


def feature_kernel(fg, k1, sums, out, classes, bias, fgw, k1t):
    classes[...] = sums[0:3, :]
    bias[...] = sums[3:4, 0:3]
    flip(k1, k1t)

    def widen(t, c):
        store_wide(fgw, t * (2 * COLS), load_rows(fg, t * (2 * COLS), 2))
        return c

    lax.fori_loop(0, 9, widen, 0)

    def step(t, c):
        at = t * (8 * COLS)
        v = conv_rows(fgw, at, 8, k1t)
        out[pl.ds(aligned(at), 8 * COLS), :] = v.astype(BF16).reshape(8 * COLS, CH)
        return c

    lax.fori_loop(0, 2, step, 0)


def convert_out(block, wide, out, sems):
    copies = []
    for t in range(6):
        at = pl.ds(t * 384, 384)
        wide[at, :] = block[at, :].astype(F32)
        copies.append(pltpu.make_async_copy(wide.at[at], out.at[at], sems.at[t]))
        copies[-1].start()
    for copy in copies:
        copy.wait()


def mine_kernel(mine, g1, g2, wide, sems):
    core = lax.axis_index("c")

    @pl.when(core == 0)
    def _():
        convert_out(mine, wide, g1, sems)

    @pl.when(core == 1)
    def _():
        convert_out(mine, wide, g2, sems)


def other_kernel(other, g1_in, g2_in, g1, g2, wide, sems):
    mine_kernel(other, g2, g1, wide, sems)


def ring(step):
    def place(z):
        return (z % 4) * 2 + z // 4

    return [(place(z), place((z + step) % 8)) for z in range(8)]


def shift(value, axis, step, size):
    return lax.ppermute(value, axis, [(i, (i + step) % size) for i in range(size)])


def split_small(small):
    hi = small.astype(BF16)
    return jnp.concatenate([hi, (small - hi.astype(F32)).astype(BF16)], axis=0)


def join_small(rows):
    full = rows.astype(F32)
    return full[..., 0:4, :] + full[..., 4:8, :]


def per_device(features, first_kernel, second_kernel, classifier, class_bias, labels):
    height = ROWS * lax.axis_size(BAND)
    count = height * COLS * lax.axis_size(RAIL)
    scale = float(count) ** (-0.5)
    core = lax.axis_index("c")

    flat = features.reshape(PIX, CH)
    lab = labels.reshape(ROWS, COLS)
    k1 = first_kernel.reshape(9 * CH, CH)
    k2 = second_kernel.reshape(9 * CH, CH)
    up, down, fv, labels = call(
        edge_kernel,
        [((BLOCK, CH), BF16), ((BLOCK, CH), BF16), ((PIX, CH), BF16), ((ROWS, COLS), jnp.int32)],
        (flat, lab), [VMEM] * 2, [pltpu.VMEM((16, CH), F32)], limit=8, name="edge",
    )
    first = core == 0
    up, down, first = lax.optimization_barrier((up, down, first))
    above = lax.ppermute(down, DEPTH, ring(1))
    below = lax.ppermute(up, DEPTH, ring(7))

    fwi, awi, slopei, k2t = call(
        inner_kernel,
        [((PIX, 3 * CH), BF16), ((14 * COLS, 3 * CH), BF16), ((14 * COLS, CH), F32),
         ((9 * CH, CH), BF16)],
        (fv, k1, k2), [VMEM] * 3,
        flops=5_000_000_000, limit=12, name="inner",
    )

    g1, g2, small, fg = call(
        make_main(height, scale),
        [((9 * CH, CH), BF16), ((9 * CH, CH), BF16), ((8, CH), F32), ((18 * COLS, CH), BF16)],
        (class_bias.reshape(1, 3), above, below, fwi, awi, slopei, k1, k2, k2t, classifier.T, labels),
        [VMEM] * 11,
        [
            pltpu.VMEM((24 * COLS, 3 * CH), BF16),
            pltpu.VMEM((22 * COLS, 3 * CH), BF16),
            pltpu.VMEM((20 * COLS, 3 * CH), BF16),
            pltpu.VMEM((18 * COLS, 3 * CH), BF16),
            pltpu.VMEM((CH, PIX), BF16),
            pltpu.VMEM((22 * COLS, CH), F32),
            pltpu.VMEM((20 // R2, 8, 1024), F32),
            pltpu.VMEM((2, R2 * COLS, CH), F32),
            pltpu.VMEM((16, CH), F32),
            pltpu.VMEM((16, CH), BF16),
        ],
        limit=22, flops=9_000_000_000, name="main",
    )
    small = small[0:4]
    keep = jnp.where(first, g1, g2)
    give = jnp.where(first, g2, g1)
    tail = jnp.pad(split_small(small), ((0, 8), (0, 0)))
    got = shift(jnp.concatenate([give, tail], axis=0), "c", 1, 2)
    total = (keep.astype(F32) + got[:9 * CH].astype(F32)).astype(BF16)
    small = small + join_small(got[9 * CH:])

    part = 9 * CH // 32
    spread = jnp.concatenate(
        [total.reshape(32, part, CH), jnp.broadcast_to(split_small(small), (32, 8, CH))], axis=1
    )
    spread = lax.all_to_all(spread, PLANE, 0, 0, tiled=True)
    piece = jnp.sum(spread[:, :part].astype(F32), axis=0).astype(BF16)
    small = jnp.sum(join_small(spread[:, part:]), axis=0)

    send = jnp.concatenate([piece, split_small(small)], axis=0)
    one, two, three = [lax.ppermute(send, DEPTH, ring(k)) for k in (2, 4, 6)]

    def four(mine, pick):
        return (mine + pick(two)) + (pick(one) + pick(three))

    small = four(small, lambda block: join_small(block[part:]))
    piece = four(piece.astype(F32), lambda block: block[:part].astype(F32)).astype(BF16)

    grad_features, grad_classifier, grad_bias = call(
        feature_kernel, [((PIX, CH), BF16), ((3, CH), F32), ((1, 3), F32)], (fg, k1, small), [VMEM] * 3,
        [pltpu.VMEM((18 * COLS, 3 * CH), BF16), pltpu.VMEM((9 * CH, CH), BF16)],
        limit=12, flops=2_500_000_000, name="feature",
    )
    full = lax.all_to_all(jnp.broadcast_to(piece, (32, part, CH)), PLANE, 0, 0, tiled=True)
    full, grad_features = lax.optimization_barrier((full, grad_features))
    mine = full.reshape(9 * CH, CH)
    other = shift(mine, "c", 1, 2)
    outs = [((9 * CH, CH), F32)] * 2
    scratch = [pltpu.VMEM((9 * CH, CH), F32), pltpu.SemaphoreType.DMA((6,))]
    halves = call(
        mine_kernel, outs, (mine,), [VMEM], scratch,
        limit=8, flops=1_000_000_000, name="mine", out_specs=(HBM, HBM),
    )
    grad_first, grad_second = call(
        other_kernel, outs, (other, *halves), [VMEM, HBM, HBM], scratch,
        limit=8, name="other", out_specs=(HBM, HBM), aliases={1: 0, 2: 1},
    )
    shape = (3, 3, CH, CH)
    return (
        grad_features.reshape(features.shape), grad_first.reshape(shape), grad_second.reshape(shape),
        grad_classifier.T, grad_bias[0],
    )


def solution(mesh):
    fine = Mesh(mesh.devices.reshape(2, 2, 4, 2, 4, 2), AXES)
    pixels = P(RAIL, BAND, None, None)
    placed = (pixels, P(), P(), P(), P(), P(RAIL, BAND, None))
    return jax.shard_map(
        per_device,
        mesh=fine,
        in_specs=placed,
        out_specs=(pixels, P(), P(), P(), P()),
        check_vma=False,
    )
```

```python
import jax
import jax.numpy as jnp
from jax import lax
from jax.experimental import pallas as pl
from jax.experimental.pallas import tpu as pltpu
from jax.sharding import Mesh, PartitionSpec as P

ROWS = 16
COLS = 96
CH = 256
HALO = 4
PIX = ROWS * COLS
EDGE = HALO * COLS
BLOCK = EDGE + 16
HALF = 9 * CH // 2
R2 = 10
F32 = jnp.float32
BF16 = jnp.bfloat16
ROWWISE = (((0,), (0,)), ((), ()))
VMEM = pl.BlockSpec(memory_space=pltpu.VMEM)
HBM = pl.BlockSpec(memory_space=pltpu.HBM)
AXES = ("q", "p", "x", "h", "y", "c")
BAND = ("q", "p")
DEPTH = ("q", "p", "h")
PLANE = ("p", "x", "y")
RAIL = ("x", "h", "y", "c")


def call(kernel, outs, args, ins, scratch=(), limit=24, flops=0, name=None, out_specs=None, aliases={}):
    moved = sum(a.size * a.dtype.itemsize for a in args)
    shapes = tuple(jax.ShapeDtypeStruct(s, d) for s, d in outs)
    return pl.pallas_call(
        kernel,
        out_shape=shapes,
        in_specs=list(ins),
        input_output_aliases=aliases,
        out_specs=(VMEM,) * len(outs) if out_specs is None else out_specs,
        scratch_shapes=list(scratch),
        compiler_params=pltpu.CompilerParams(vmem_limit_bytes=limit * 1024 * 1024),
        cost_estimate=pl.CostEstimate(flops=flops, bytes_accessed=moved, transcendentals=0),
        name=name,
    )(*args)


def aligned(start):
    return start if isinstance(start, int) else pl.multiple_of(start, COLS)


def conv_rows(wide, start, count, kernel):
    patch = jnp.concatenate(
        [wide[pl.ds(aligned(start + a * COLS), count * COLS), :] for a in range(3)], axis=1
    )
    out = jnp.dot(patch, kernel[...], preferred_element_type=F32)
    return out.reshape(count, COLS, CH)


def store_wide(wide, start, rows):
    count = rows.shape[0]
    col = lax.broadcasted_iota(jnp.int32, rows.shape, 1)
    left = jnp.where(col == 0, 0.0, pltpu.roll(rows, 1, 1))
    right = jnp.where(col == COLS - 1, 0.0, pltpu.roll(rows, COLS - 1, 1))
    at = pl.ds(aligned(start), count * COLS)
    wide[at, 0:CH] = left.astype(BF16).reshape(count * COLS, CH)
    wide[at, CH:2 * CH] = rows.astype(BF16).reshape(count * COLS, CH)
    wide[at, 2 * CH:3 * CH] = right.astype(BF16).reshape(count * COLS, CH)


def load_rows(ref, start, count):
    at = pl.ds(aligned(start), count * COLS)
    return ref[at, :].astype(F32).reshape(count, COLS, CH)


def sigmoid(value):
    return 0.5 * jnp.tanh(0.5 * value) + 0.5


def keep_rows(rows, first, height):
    parts = []
    for r in range(rows.shape[0]):
        inside = jnp.logical_and(first + r >= 0, first + r < height)
        parts.append(rows[r] * jnp.where(inside, 1.0, 0.0))
    return jnp.stack(parts)


def edge_kernel(f, lab, up, down, fv, tag):
    for out, row, label in ((up, 0, 0), (down, ROWS - HALO, ROWS - 2)):
        out[0:EDGE, :] = f[row * COLS:(row + HALO) * COLS, :]
        tag[...] = jnp.zeros_like(tag)
        tag[0:2, 0:COLS] = lab[label:label + 2, :].astype(F32)
        out[EDGE:BLOCK, :] = tag[...].astype(BF16)
    fv[...] = f[...]


def flip(src, dst):
    for t in range(9):
        dst[t * CH:(t + 1) * CH, :] = src[(8 - t) * CH:(9 - t) * CH, :].T


def inner_kernel(f, k1, k2, fw, aw, slope, k2t):
    def widen(t, c):
        store_wide(fw, t * (2 * COLS), load_rows(f, t * (2 * COLS), 2))
        return c

    lax.fori_loop(0, 8, widen, 0)

    for t in range(7):
        at = t * (2 * COLS)
        v = conv_rows(fw, at, 2, k1)
        s = sigmoid(v)
        slope[pl.ds(at, 2 * COLS), :] = (s * (1.0 + v * (1.0 - s))).reshape(2 * COLS, CH)
        store_wide(aw, at, v * s)

    flip(k2, k2t)


def weight_grad(grad_wide, skip, src, src_skip, out, gt):
    gt[...] = grad_wide[skip * COLS:(skip + ROWS) * COLS, CH:2 * CH].T
    for a in range(3):
        win = src[(src_skip + a) * COLS:(src_skip + a + ROWS) * COLS, :]
        res = jnp.dot(gt[...], win, preferred_element_type=F32)
        for b in range(3):
            out[(3 * a + b) * CH:(3 * a + b + 1) * CH, :] = (
                res[:, b * CH:(b + 1) * CH].T.astype(BF16)
            )


def band_start():
    return (lax.axis_index("q") * 2 + lax.axis_index("p")) * ROWS


def make_upper(height, scale):
    def upper(bias, above, below, fwi, awi, k1, k2, classes, lab, g2, small, sw, slope,
              fw, aw, gt, labs, held, cls32, cls):
        base = band_start()
        cls32[...] = jnp.zeros_like(cls32)
        cls32[0:3, :] = classes[...].astype(F32)
        cls32[3:6, :] = classes[...].astype(F32)
        cls[...] = cls32[...].astype(BF16)
        fw[4 * COLS:6 * COLS, :] = fwi[0:2 * COLS, :]
        fw[6 * COLS:8 * COLS, :] = fwi[14 * COLS:16 * COLS, :]
        for half in range(2):
            at = half * 2 * COLS
            rows = keep_rows(load_rows(above, at, 2), base - HALO + half * 2, height)
            store_wide(fw, at, rows)
            rows = keep_rows(load_rows(below, at, 2), base + ROWS + half * 2, height)
            store_wide(fw, 8 * COLS + at, rows)
        aw[4 * COLS:18 * COLS, :] = awi[...]

        tags = [above[EDGE:BLOCK, :].astype(F32), below[EDGE:BLOCK, :].astype(F32)]
        mine = lab[...].astype(F32)
        lines = [tags[0][0:1, 0:COLS], tags[0][1:2, 0:COLS]]
        lines += [mine[r:r + 1, :] for r in range(ROWS)]
        lines += [tags[1][0:1, 0:COLS], tags[1][1:2, 0:COLS]]
        for r, line in enumerate(lines):
            labs[r // R2, 0:1, (r % R2) * COLS:(r % R2 + 1) * COLS] = line

        for t in range(2):
            v = conv_rows(fw, t * (6 * COLS), 4, k1)
            s = sigmoid(v)
            slope[t * 4 * COLS:(t + 1) * 4 * COLS, :] = (
                s * (1.0 + v * (1.0 - s))
            ).reshape(4 * COLS, CH)
            store_wide(aw, t * (18 * COLS), keep_rows(v * s, base - 3 + t * 18, height))

        small[...] = jnp.zeros_like(small)
        lane = lax.broadcasted_iota(jnp.int32, (1, CH), 1)
        pixel = lax.broadcasted_iota(jnp.int32, (1, R2 * COLS), 1)

        def wide_act(t):
            held[t % 2, :, :] = conv_rows(aw, t * (R2 * COLS), R2, k2).reshape(R2 * COLS, CH)

        def second(t):
            at = t * (R2 * COLS)
            v = held[t % 2, :, :].reshape(R2, COLS, CH)
            s = sigmoid(v)
            act = (v * s).astype(BF16).reshape(R2 * COLS, CH)
            logit = lax.dot_general(
                cls[...], act, (((1,), (1,)), ((), ())), preferred_element_type=F32
            )
            rows = [logit[k:k + 1, :] + bias[0:1, k:k + 1] for k in range(3)]
            top = jnp.maximum(jnp.maximum(rows[0], rows[1]), rows[2])
            ex = [jnp.exp(row - top) for row in rows]
            den = ex[0] + ex[1] + ex[2]
            label = labs[t, 0:1, 0:R2 * COLS]
            place = pixel + at
            own = jnp.where(jnp.logical_and(place >= 2 * COLS, place < 18 * COLS), 1.0, 0.0)
            dl = [(ex[k] / den - jnp.where(label == k, 1.0, 0.0)) * scale for k in range(3)]
            hi = [d.astype(BF16).astype(F32) for d in dl]
            lo = [d - h for d, h in zip(dl, hi)]
            zero = jnp.zeros((10, R2 * COLS), F32)
            pack = jnp.concatenate(hi + lo + [zero], axis=0)
            back = lax.dot_general(pack.astype(BF16), cls[...], ROWWISE, preferred_element_type=F32)
            grad = back.reshape(R2, COLS, CH) * (s * (1.0 + v * (1.0 - s)))
            store_wide(sw, at, keep_rows(grad, base - 2 + t * R2, height))
            part = jnp.dot((pack * own).astype(BF16), act, preferred_element_type=F32)
            sums = [jnp.sum(d * own, axis=1, keepdims=True) for d in dl]
            row = jnp.where(lane == 0, sums[0], jnp.where(lane == 1, sums[1], 0.0))
            small[0:3, :] += part[0:3] + part[3:6]
            small[3:4, :] += jnp.where(lane == 2, sums[2], row)

        N2 = 20 // R2
        for t in range(N2 + 1):
            if t < N2:
                wide_act(t)
            if t > 0:
                second(t - 1)

        weight_grad(sw, 2, aw, 2, g2, gt)

    return upper


def make_lower(height):
    def lower(above, below, fwi, slopei, slope_ends, sw, k2t, g1, fg, fw, fgw, gt, slope):
        base = band_start()
        fw[COLS:17 * COLS, :] = fwi[...]
        store_wide(fw, 0, keep_rows(load_rows(above, 3 * COLS, 1), base - 1, height))
        store_wide(fw, 17 * COLS, keep_rows(load_rows(below, 0, 1), base + ROWS, height))
        slope[0:2 * COLS, :] = slope_ends[2 * COLS:4 * COLS, :]
        slope[2 * COLS:16 * COLS, :] = slopei[...]
        slope[16 * COLS:18 * COLS, :] = slope_ends[4 * COLS:6 * COLS, :]
        for t in range(6):
            at = t * (3 * COLS)
            v = conv_rows(sw, at, 3, k2t)
            g = keep_rows(v * load_rows(slope, at, 3), base - 1 + t * 3, height)
            store_wide(fgw, at, g)
        weight_grad(fgw, 1, fw, 0, g1, gt)
        fg[...] = fgw[:, CH:2 * CH]

    return lower


def feature_kernel(fg, k1, sums, out, classes, bias, fgw, k1t):
    classes[...] = sums[0:3, :]
    bias[...] = sums[3:4, 0:3]
    flip(k1, k1t)

    def widen(t, c):
        store_wide(fgw, t * (2 * COLS), load_rows(fg, t * (2 * COLS), 2))
        return c

    lax.fori_loop(0, 9, widen, 0)

    def step(t, c):
        at = t * (8 * COLS)
        v = conv_rows(fgw, at, 8, k1t)
        out[pl.ds(aligned(at), 8 * COLS), :] = v.astype(BF16).reshape(8 * COLS, CH)
        return c

    lax.fori_loop(0, 2, step, 0)


def convert_out(block, owner, g1, g2, wide, sems):
    copies = []
    for t in range(6):
        at = pl.ds(t * 384, 384)
        out = g1 if t < 3 else g2
        row = pl.multiple_of(owner * HALF + (t % 3) * 384, 384)
        wide[at, :] = block[at, :].astype(F32)
        copies.append(pltpu.make_async_copy(wide.at[at], out.at[pl.ds(row, 384)], sems.at[t]))
        copies[-1].start()
    for copy in copies:
        copy.wait()


def mine_kernel(mine, g1, g2, wide, sems):
    convert_out(mine, lax.axis_index("c"), g1, g2, wide, sems)


def other_kernel(other, g1_in, g2_in, g1, g2, wide, sems):
    convert_out(other, 1 - lax.axis_index("c"), g1, g2, wide, sems)


def ring(step):
    def place(z):
        return (z % 4) * 2 + z // 4

    return [(place(z), place((z + step) % 8)) for z in range(8)]


def shift(value, axis, step, size):
    return lax.ppermute(value, axis, [(i, (i + step) % size) for i in range(size)])


def halves(first, grad):
    low, high = grad[:HALF], grad[HALF:]
    return jnp.where(first, low, high), jnp.where(first, high, low)


def split_small(small):
    hi = small.astype(BF16)
    return jnp.concatenate([hi, (small - hi.astype(F32)).astype(BF16)], axis=0)


def join_small(rows):
    full = rows.astype(F32)
    return full[..., 0:4, :] + full[..., 4:8, :]


def per_device(features, first_kernel, second_kernel, classifier, class_bias, labels):
    height = ROWS * lax.axis_size(BAND)
    count = height * COLS * lax.axis_size(RAIL)
    scale = float(count) ** (-0.5)
    core = lax.axis_index("c")

    flat = features.reshape(PIX, CH)
    lab = labels.reshape(ROWS, COLS)
    k1 = first_kernel.reshape(9 * CH, CH)
    k2 = second_kernel.reshape(9 * CH, CH)
    up, down, fv = call(
        edge_kernel,
        [((BLOCK, CH), BF16), ((BLOCK, CH), BF16), ((PIX, CH), BF16)],
        (flat, lab), [VMEM] * 2, [pltpu.VMEM((16, CH), F32)], limit=8, name="edge",
    )
    first = core == 0
    up, down, first = lax.optimization_barrier((up, down, first))
    above = lax.ppermute(down, DEPTH, ring(1))
    below = lax.ppermute(up, DEPTH, ring(7))

    fwi, awi, slopei, k2t = call(
        inner_kernel,
        [((PIX, 3 * CH), BF16), ((14 * COLS, 3 * CH), BF16), ((14 * COLS, CH), F32),
         ((9 * CH, CH), BF16)],
        (fv, k1, k2), [VMEM] * 3,
        flops=5_000_000_000, limit=12, name="inner",
    )

    g2, small, sw, slope_ends = call(
        make_upper(height, scale),
        [((9 * CH, CH), BF16), ((8, CH), F32), ((20 * COLS, 3 * CH), BF16), ((8 * COLS, CH), F32)],
        (class_bias.reshape(1, 3), above, below, fwi, awi, k1, k2, classifier.T, lab), [VMEM] * 9,
        [
            pltpu.VMEM((12 * COLS, 3 * CH), BF16),
            pltpu.VMEM((22 * COLS, 3 * CH), BF16),
            pltpu.VMEM((CH, PIX), BF16),
            pltpu.VMEM((20 // R2, 8, 1024), F32),
            pltpu.VMEM((2, R2 * COLS, CH), F32),
            pltpu.VMEM((16, CH), F32),
            pltpu.VMEM((16, CH), BF16),
        ],
        limit=18, flops=6_000_000_000, name="upper",
    )
    small = small[0:4]
    keep, give = halves(first, g2)
    tail = jnp.pad(split_small(small), ((0, 8), (0, 0)))
    got = shift(jnp.concatenate([give, tail], axis=0), "c", 1, 2)
    g1, fg = call(
        make_lower(height), [((9 * CH, CH), BF16), ((18 * COLS, CH), BF16)],
        (above, below, fwi, slopei, slope_ends, sw, k2t), [VMEM] * 7,
        [
            pltpu.VMEM((18 * COLS, 3 * CH), BF16),
            pltpu.VMEM((18 * COLS, 3 * CH), BF16),
            pltpu.VMEM((CH, PIX), BF16),
            pltpu.VMEM((18 * COLS, CH), F32),
        ],
        limit=18, flops=4_000_000_000, name="lower",
    )
    total_second = (keep.astype(F32) + got[:HALF].astype(F32)).astype(BF16)
    small = small + join_small(got[HALF:])
    keep, give = halves(first, g1)
    total_first = (keep.astype(F32) + shift(give, "c", 1, 2).astype(F32)).astype(BF16)
    total = jnp.concatenate([total_first, total_second], axis=0)

    part = 9 * CH // 32
    spread = jnp.concatenate(
        [total.reshape(32, part, CH), jnp.broadcast_to(split_small(small), (32, 8, CH))], axis=1
    )
    spread = lax.all_to_all(spread, PLANE, 0, 0, tiled=True)
    piece = jnp.sum(spread[:, :part].astype(F32), axis=0).astype(BF16)
    small = jnp.sum(join_small(spread[:, part:]), axis=0)

    send = jnp.concatenate([piece, split_small(small)], axis=0)
    one, two, three = [lax.ppermute(send, DEPTH, ring(k)) for k in (2, 4, 6)]

    def four(mine, pick):
        return (mine + pick(two)) + (pick(one) + pick(three))

    small = four(small, lambda block: join_small(block[part:]))
    piece = four(piece.astype(F32), lambda block: block[:part].astype(F32)).astype(BF16)

    grad_features, grad_classifier, grad_bias = call(
        feature_kernel, [((PIX, CH), BF16), ((3, CH), F32), ((1, 3), F32)], (fg, k1, small), [VMEM] * 3,
        [pltpu.VMEM((18 * COLS, 3 * CH), BF16), pltpu.VMEM((9 * CH, CH), BF16)],
        limit=12, flops=2_500_000_000, name="feature",
    )
    full = lax.all_to_all(jnp.broadcast_to(piece, (32, part, CH)), PLANE, 0, 0, tiled=True)
    full, grad_features = lax.optimization_barrier((full, grad_features))
    mine = full.reshape(9 * CH, CH)
    other = shift(mine, "c", 1, 2)
    outs = [((9 * CH, CH), F32)] * 2
    scratch = [pltpu.VMEM((9 * CH, CH), F32), pltpu.SemaphoreType.DMA((6,))]
    parts = call(
        mine_kernel, outs, (mine,), [VMEM], scratch,
        limit=8, flops=1_000_000_000, name="mine", out_specs=(HBM, HBM),
    )
    grad_first, grad_second = call(
        other_kernel, outs, (other, *parts), [VMEM, HBM, HBM], scratch,
        limit=8, name="other", out_specs=(HBM, HBM), aliases={1: 0, 2: 1},
    )
    shape = (3, 3, CH, CH)
    return (
        grad_features.reshape(features.shape), grad_first.reshape(shape), grad_second.reshape(shape),
        grad_classifier.T, grad_bias[0],
    )


def solution(mesh):
    fine = Mesh(mesh.devices.reshape(2, 2, 4, 2, 4, 2), AXES)
    pixels = P(RAIL, BAND, None, None)
    placed = (pixels, P(), P(), P(), P(), P(RAIL, BAND, None))
    return jax.shard_map(
        per_device,
        mesh=fine,
        in_specs=placed,
        out_specs=(pixels, P(), P(), P(), P()),
        check_vma=False,
    )
```

```python
import jax
import jax.numpy as jnp
from jax import lax
from jax.experimental import pallas as pl
from jax.experimental.pallas import tpu as pltpu
from jax.sharding import Mesh, PartitionSpec as P

ROWS = 16
COLS = 96
CH = 256
HALO = 4
PIX = ROWS * COLS
EDGE = HALO * COLS
BLOCK = EDGE + 16
HALF = 9 * CH // 2
R2 = 10
F32 = jnp.float32
BF16 = jnp.bfloat16
ROWWISE = (((0,), (0,)), ((), ()))
VMEM = pl.BlockSpec(memory_space=pltpu.VMEM)
HBM = pl.BlockSpec(memory_space=pltpu.HBM)
AXES = ("q", "p", "x", "h", "y", "c")
BAND = ("q", "p")
DEPTH = ("q", "p", "h")
PLANE = ("p", "x", "y")
RAIL = ("x", "h", "y", "c")


def call(kernel, outs, args, ins, scratch=(), limit=24, flops=0, name=None, out_specs=None, aliases={}):
    moved = sum(a.size * a.dtype.itemsize for a in args)
    shapes = tuple(jax.ShapeDtypeStruct(s, d) for s, d in outs)
    return pl.pallas_call(
        kernel,
        out_shape=shapes,
        in_specs=list(ins),
        input_output_aliases=aliases,
        out_specs=(VMEM,) * len(outs) if out_specs is None else out_specs,
        scratch_shapes=list(scratch),
        compiler_params=pltpu.CompilerParams(vmem_limit_bytes=limit * 1024 * 1024),
        cost_estimate=pl.CostEstimate(flops=flops, bytes_accessed=moved, transcendentals=0),
        name=name,
    )(*args)


def aligned(start):
    return start if isinstance(start, int) else pl.multiple_of(start, COLS)


def conv_rows(wide, start, count, kernel):
    patch = jnp.concatenate(
        [wide[pl.ds(aligned(start + a * COLS), count * COLS), :] for a in range(3)], axis=1
    )
    out = jnp.dot(patch, kernel[...], preferred_element_type=F32)
    return out.reshape(count, COLS, CH)


def store_wide(wide, start, rows):
    count = rows.shape[0]
    col = lax.broadcasted_iota(jnp.int32, rows.shape, 1)
    left = jnp.where(col == 0, 0.0, pltpu.roll(rows, 1, 1))
    right = jnp.where(col == COLS - 1, 0.0, pltpu.roll(rows, COLS - 1, 1))
    at = pl.ds(aligned(start), count * COLS)
    wide[at, 0:CH] = left.astype(BF16).reshape(count * COLS, CH)
    wide[at, CH:2 * CH] = rows.astype(BF16).reshape(count * COLS, CH)
    wide[at, 2 * CH:3 * CH] = right.astype(BF16).reshape(count * COLS, CH)


def load_rows(ref, start, count):
    at = pl.ds(aligned(start), count * COLS)
    return ref[at, :].astype(F32).reshape(count, COLS, CH)


def sigmoid(value):
    return 0.5 * jnp.tanh(0.5 * value) + 0.5


def keep_rows(rows, first, height):
    parts = []
    for r in range(rows.shape[0]):
        inside = jnp.logical_and(first + r >= 0, first + r < height)
        parts.append(rows[r] * jnp.where(inside, 1.0, 0.0))
    return jnp.stack(parts)


def edge_kernel(f, lab, up, down, fv, tag):
    for out, row, label in ((up, 0, 0), (down, ROWS - HALO, ROWS - 2)):
        out[0:EDGE, :] = f[row * COLS:(row + HALO) * COLS, :]
        tag[...] = jnp.zeros_like(tag)
        tag[0:2, 0:COLS] = lab[label:label + 2, :].astype(F32)
        out[EDGE:BLOCK, :] = tag[...].astype(BF16)
    fv[...] = f[...]


def flip(src, dst):
    for t in range(9):
        dst[t * CH:(t + 1) * CH, :] = src[(8 - t) * CH:(9 - t) * CH, :].T


def inner_kernel(f, k1, k2, fw, aw, slope, k2t):
    def widen(t, c):
        store_wide(fw, t * (2 * COLS), load_rows(f, t * (2 * COLS), 2))
        return c

    lax.fori_loop(0, 8, widen, 0)

    for t in range(7):
        at = t * (2 * COLS)
        v = conv_rows(fw, at, 2, k1)
        s = sigmoid(v)
        slope[pl.ds(at, 2 * COLS), :] = (s * (1.0 + v * (1.0 - s))).reshape(2 * COLS, CH)
        store_wide(aw, at, v * s)

    flip(k2, k2t)


def weight_grad(grad_wide, skip, src, src_skip, out, gt):
    gt[...] = grad_wide[skip * COLS:(skip + ROWS) * COLS, CH:2 * CH].T
    for a in range(3):
        win = src[(src_skip + a) * COLS:(src_skip + a + ROWS) * COLS, :]
        res = jnp.dot(gt[...], win, preferred_element_type=F32)
        for b in range(3):
            out[(3 * a + b) * CH:(3 * a + b + 1) * CH, :] = (
                res[:, b * CH:(b + 1) * CH].T.astype(BF16)
            )


def band_start():
    return (lax.axis_index("q") * 2 + lax.axis_index("p")) * ROWS


def make_upper(height, scale):
    def upper(bias, above, below, fwi, awi, k1, k2, classes, lab, g2, small, sw, slope,
              fw, aw, gt, labs, held, cls32, cls):
        base = band_start()
        cls32[...] = jnp.zeros_like(cls32)
        cls32[0:3, :] = classes[...].astype(F32)
        cls32[3:6, :] = classes[...].astype(F32)
        cls[...] = cls32[...].astype(BF16)
        fw[4 * COLS:6 * COLS, :] = fwi[0:2 * COLS, :]
        fw[6 * COLS:8 * COLS, :] = fwi[14 * COLS:16 * COLS, :]
        for half in range(2):
            at = half * 2 * COLS
            rows = keep_rows(load_rows(above, at, 2), base - HALO + half * 2, height)
            store_wide(fw, at, rows)
            rows = keep_rows(load_rows(below, at, 2), base + ROWS + half * 2, height)
            store_wide(fw, 8 * COLS + at, rows)
        aw[4 * COLS:18 * COLS, :] = awi[...]

        tags = [above[EDGE:BLOCK, :].astype(F32), below[EDGE:BLOCK, :].astype(F32)]
        mine = lab[...].astype(F32)
        lines = [tags[0][0:1, 0:COLS], tags[0][1:2, 0:COLS]]
        lines += [mine[r:r + 1, :] for r in range(ROWS)]
        lines += [tags[1][0:1, 0:COLS], tags[1][1:2, 0:COLS]]
        for r, line in enumerate(lines):
            labs[r // R2, 0:1, (r % R2) * COLS:(r % R2 + 1) * COLS] = line

        for t in range(2):
            v = conv_rows(fw, t * (6 * COLS), 4, k1)
            s = sigmoid(v)
            slope[t * 4 * COLS:(t + 1) * 4 * COLS, :] = (
                s * (1.0 + v * (1.0 - s))
            ).reshape(4 * COLS, CH)
            store_wide(aw, t * (18 * COLS), keep_rows(v * s, base - 3 + t * 18, height))

        small[...] = jnp.zeros_like(small)
        lane = lax.broadcasted_iota(jnp.int32, (1, CH), 1)
        pixel = lax.broadcasted_iota(jnp.int32, (1, R2 * COLS), 1)

        def wide_act(t):
            held[t % 2, :, :] = conv_rows(aw, t * (R2 * COLS), R2, k2).reshape(R2 * COLS, CH)

        def second(t):
            at = t * (R2 * COLS)
            v = held[t % 2, :, :].reshape(R2, COLS, CH)
            s = sigmoid(v)
            act = (v * s).astype(BF16).reshape(R2 * COLS, CH)
            logit = lax.dot_general(
                cls[...], act, (((1,), (1,)), ((), ())), preferred_element_type=F32
            )
            rows = [logit[k:k + 1, :] + bias[0:1, k:k + 1] for k in range(3)]
            top = jnp.maximum(jnp.maximum(rows[0], rows[1]), rows[2])
            ex = [jnp.exp(row - top) for row in rows]
            den = ex[0] + ex[1] + ex[2]
            label = labs[t, 0:1, 0:R2 * COLS]
            place = pixel + at
            own = jnp.where(jnp.logical_and(place >= 2 * COLS, place < 18 * COLS), 1.0, 0.0)
            dl = [(ex[k] / den - jnp.where(label == k, 1.0, 0.0)) * scale for k in range(3)]
            hi = [d.astype(BF16).astype(F32) for d in dl]
            lo = [d - h for d, h in zip(dl, hi)]
            zero = jnp.zeros((10, R2 * COLS), F32)
            pack = jnp.concatenate(hi + lo + [zero], axis=0)
            back = lax.dot_general(pack.astype(BF16), cls[...], ROWWISE, preferred_element_type=F32)
            grad = back.reshape(R2, COLS, CH) * (s * (1.0 + v * (1.0 - s)))
            store_wide(sw, at, keep_rows(grad, base - 2 + t * R2, height))
            part = jnp.dot((pack * own).astype(BF16), act, preferred_element_type=F32)
            sums = [jnp.sum(d * own, axis=1, keepdims=True) for d in dl]
            row = jnp.where(lane == 0, sums[0], jnp.where(lane == 1, sums[1], 0.0))
            small[0:3, :] += part[0:3] + part[3:6]
            small[3:4, :] += jnp.where(lane == 2, sums[2], row)

        N2 = 20 // R2
        for t in range(N2 + 1):
            if t < N2:
                wide_act(t)
            if t > 0:
                second(t - 1)

        weight_grad(sw, 2, aw, 2, g2, gt)

    return upper


def make_lower(height):
    def lower(above, below, fwi, slopei, slope_ends, sw, k2t, g1, fg, fw, fgw, gt, slope):
        base = band_start()
        fw[COLS:17 * COLS, :] = fwi[...]
        store_wide(fw, 0, keep_rows(load_rows(above, 3 * COLS, 1), base - 1, height))
        store_wide(fw, 17 * COLS, keep_rows(load_rows(below, 0, 1), base + ROWS, height))
        slope[0:2 * COLS, :] = slope_ends[2 * COLS:4 * COLS, :]
        slope[2 * COLS:16 * COLS, :] = slopei[...]
        slope[16 * COLS:18 * COLS, :] = slope_ends[4 * COLS:6 * COLS, :]
        for t in range(6):
            at = t * (3 * COLS)
            v = conv_rows(sw, at, 3, k2t)
            g = keep_rows(v * load_rows(slope, at, 3), base - 1 + t * 3, height)
            store_wide(fgw, at, g)
        weight_grad(fgw, 1, fw, 0, g1, gt)
        fg[...] = fgw[:, CH:2 * CH]

    return lower


def feature_kernel(fg, k1, sums, out, classes, bias, fgw, k1t):
    classes[...] = sums[0:3, :]
    bias[...] = sums[3:4, 0:3]
    flip(k1, k1t)

    def widen(t, c):
        store_wide(fgw, t * (2 * COLS), load_rows(fg, t * (2 * COLS), 2))
        return c

    lax.fori_loop(0, 9, widen, 0)

    def step(t, c):
        at = t * (8 * COLS)
        v = conv_rows(fgw, at, 8, k1t)
        out[pl.ds(aligned(at), 8 * COLS), :] = v.astype(BF16).reshape(8 * COLS, CH)
        return c

    lax.fori_loop(0, 2, step, 0)


def convert_out(block, owner, g1, g2, wide, sems):
    copies = []
    for t in range(6):
        at = pl.ds(t * 384, 384)
        out = g1 if t < 3 else g2
        row = pl.multiple_of(owner * HALF + (t % 3) * 384, 384)
        wide[at, :] = block[at, :].astype(F32)
        copies.append(pltpu.make_async_copy(wide.at[at], out.at[pl.ds(row, 384)], sems.at[t]))
        copies[-1].start()
    for copy in copies:
        copy.wait()


def mine_kernel(mine, g1, g2, wide, sems):
    convert_out(mine, lax.axis_index("c"), g1, g2, wide, sems)


def other_kernel(block, _, out, wide, sems):
    owner = 1 - lax.axis_index("c")
    copies = []
    for t in range(3):
        at = pl.ds(t * 384, 384)
        row = pl.multiple_of(owner * HALF + t * 384, 384)
        wide[at, :] = block[at, :].astype(F32)
        copies.append(pltpu.make_async_copy(wide.at[at], out.at[pl.ds(row, 384)], sems.at[t]))
        copies[-1].start()
    for copy in copies:
        copy.wait()


def ring(step):
    def place(z):
        return (z % 4) * 2 + z // 4

    return [(place(z), place((z + step) % 8)) for z in range(8)]


def shift(value, axis, step, size):
    return lax.ppermute(value, axis, [(i, (i + step) % size) for i in range(size)])


def halves(first, grad):
    low, high = grad[:HALF], grad[HALF:]
    return jnp.where(first, low, high), jnp.where(first, high, low)


def split_small(small):
    hi = small.astype(BF16)
    return jnp.concatenate([hi, (small - hi.astype(F32)).astype(BF16)], axis=0)


def join_small(rows):
    full = rows.astype(F32)
    return full[..., 0:4, :] + full[..., 4:8, :]


def per_device(features, first_kernel, second_kernel, classifier, class_bias, labels):
    height = ROWS * lax.axis_size(BAND)
    count = height * COLS * lax.axis_size(RAIL)
    scale = float(count) ** (-0.5)
    core = lax.axis_index("c")

    flat = features.reshape(PIX, CH)
    lab = labels.reshape(ROWS, COLS)
    k1 = first_kernel.reshape(9 * CH, CH)
    k2 = second_kernel.reshape(9 * CH, CH)
    up, down, fv = call(
        edge_kernel,
        [((BLOCK, CH), BF16), ((BLOCK, CH), BF16), ((PIX, CH), BF16)],
        (flat, lab), [VMEM] * 2, [pltpu.VMEM((16, CH), F32)], limit=8, name="edge",
    )
    first = core == 0
    up, down, first = lax.optimization_barrier((up, down, first))
    above = lax.ppermute(down, DEPTH, ring(1))
    below = lax.ppermute(up, DEPTH, ring(7))

    fwi, awi, slopei, k2t = call(
        inner_kernel,
        [((PIX, 3 * CH), BF16), ((14 * COLS, 3 * CH), BF16), ((14 * COLS, CH), F32),
         ((9 * CH, CH), BF16)],
        (fv, k1, k2), [VMEM] * 3,
        flops=5_000_000_000, limit=12, name="inner",
    )

    g2, small, sw, slope_ends = call(
        make_upper(height, scale),
        [((9 * CH, CH), BF16), ((8, CH), F32), ((20 * COLS, 3 * CH), BF16), ((8 * COLS, CH), F32)],
        (class_bias.reshape(1, 3), above, below, fwi, awi, k1, k2, classifier.T, lab), [VMEM] * 9,
        [
            pltpu.VMEM((12 * COLS, 3 * CH), BF16),
            pltpu.VMEM((22 * COLS, 3 * CH), BF16),
            pltpu.VMEM((CH, PIX), BF16),
            pltpu.VMEM((20 // R2, 8, 1024), F32),
            pltpu.VMEM((2, R2 * COLS, CH), F32),
            pltpu.VMEM((16, CH), F32),
            pltpu.VMEM((16, CH), BF16),
        ],
        limit=18, flops=6_000_000_000, name="upper",
    )
    small = small[0:4]
    keep, give = halves(first, g2)
    tail = jnp.pad(split_small(small), ((0, 8), (0, 0)))
    got = shift(jnp.concatenate([give, tail], axis=0), "c", 1, 2)
    g1, fg = call(
        make_lower(height), [((9 * CH, CH), BF16), ((18 * COLS, CH), BF16)],
        (above, below, fwi, slopei, slope_ends, sw, k2t), [VMEM] * 7,
        [
            pltpu.VMEM((18 * COLS, 3 * CH), BF16),
            pltpu.VMEM((18 * COLS, 3 * CH), BF16),
            pltpu.VMEM((CH, PIX), BF16),
            pltpu.VMEM((18 * COLS, CH), F32),
        ],
        limit=18, flops=4_000_000_000, name="lower",
    )
    total_second = (keep.astype(F32) + got[:HALF].astype(F32)).astype(BF16)
    small = small + join_small(got[HALF:])
    keep, give = halves(first, g1)
    total_first = (keep.astype(F32) + shift(give, "c", 1, 2).astype(F32)).astype(BF16)
    total = jnp.concatenate([total_first, total_second], axis=0)

    part = 9 * CH // 32
    spread = jnp.concatenate(
        [total.reshape(32, part, CH), jnp.broadcast_to(split_small(small), (32, 8, CH))], axis=1
    )
    spread = lax.all_to_all(spread, PLANE, 0, 0, tiled=True)
    piece = jnp.sum(spread[:, :part].astype(F32), axis=0).astype(BF16)
    small = jnp.sum(join_small(spread[:, part:]), axis=0)

    send = jnp.concatenate([piece, split_small(small)], axis=0)
    one, two, three = [lax.ppermute(send, DEPTH, ring(k)) for k in (2, 4, 6)]

    def four(mine, pick):
        return (mine + pick(two)) + (pick(one) + pick(three))

    small = four(small, lambda block: join_small(block[part:]))
    piece = four(piece.astype(F32), lambda block: block[:part].astype(F32)).astype(BF16)

    grad_features, grad_classifier, grad_bias = call(
        feature_kernel, [((PIX, CH), BF16), ((3, CH), F32), ((1, 3), F32)], (fg, k1, small), [VMEM] * 3,
        [pltpu.VMEM((18 * COLS, 3 * CH), BF16), pltpu.VMEM((9 * CH, CH), BF16)],
        limit=12, flops=2_500_000_000, name="feature",
    )
    full = lax.all_to_all(jnp.broadcast_to(piece, (32, part, CH)), PLANE, 0, 0, tiled=True)
    full, grad_features = lax.optimization_barrier((full, grad_features))
    mine = full.reshape(9 * CH, CH)
    others = [shift(mine[k * HALF:(k + 1) * HALF], "c", 1, 2) for k in range(2)]
    outs = [((9 * CH, CH), F32)] * 2
    scratch = [pltpu.VMEM((9 * CH, CH), F32), pltpu.SemaphoreType.DMA((6,))]
    parts = call(
        mine_kernel, outs, (mine,), [VMEM], scratch,
        limit=8, flops=1_000_000_000, name="mine", out_specs=(HBM, HBM),
    )
    scratch = [pltpu.VMEM((HALF, CH), F32), pltpu.SemaphoreType.DMA((3,))]
    grad_first, grad_second = [
        call(
            other_kernel, outs[:1], (block, part_out), [VMEM, HBM], scratch,
            limit=8, name="other", out_specs=(HBM,), aliases={1: 0},
        )[0]
        for block, part_out in zip(others, parts)
    ]
    shape = (3, 3, CH, CH)
    return (
        grad_features.reshape(features.shape), grad_first.reshape(shape), grad_second.reshape(shape),
        grad_classifier.T, grad_bias[0],
    )


def solution(mesh):
    fine = Mesh(mesh.devices.reshape(2, 2, 4, 2, 4, 2), AXES)
    pixels = P(RAIL, BAND, None, None)
    placed = (pixels, P(), P(), P(), P(), P(RAIL, BAND, None))
    return jax.shard_map(
        per_device,
        mesh=fine,
        in_specs=placed,
        out_specs=(pixels, P(), P(), P(), P()),
        check_vma=False,
    )
```
